512 devices in a mesh: fsdp: 64 (over x, y, core), tp: 8 (over z).
Axes of the slice: x: 4, y: 8, z: 8, core: 2. Of those that a mesh axis runs over, the one named last changes fastest.
Arguments:
- momentum: bfloat16 [28672, 8192], P('fsdp', 'tp'), may hold values from -6 to 6
- gradient: bfloat16 [28672, 8192], P('fsdp', 'tp'), may hold values from -150 to 150, as said below
- right_factor: bfloat16 [8, 1024, 512], P('tp', 'fsdp'), may hold values from -0.0625 to 0.0625
- weight: bfloat16 [28672, 8192], P('fsdp', 'tp'), may hold values from -6 to 6
Outputs:
- momentum_new: bfloat16 [28672, 8192], P('fsdp', 'tp')
- factor_new: bfloat16 [8, 1024, 512], P('tp', 'fsdp')
- weight_new: bfloat16 [28672, 8192], P('fsdp', 'tp')
The draws below stay inside these ranges and needn't reach their ends.
Inputs may be any that keep to these rules, and one draw needn't show every extreme that they name: `gradient`: Real-valued entries.
All inputs are finite; a program needn't handle non-finite values.
Results may differ from the reference program's by a relative error of at most 0.009.
Values may be sent and summed in bfloat16 or wider, within the bound.
A program may use at most 64 MiB of HBM per device.

```python
import jax
import jax.numpy as jnp
from jax import lax

D = 8192
FF = 28672
RANK = 512
N_TP = 8


def draw_gradient(key, part):
    key = jax.random.fold_in(key, 7)
    key_rows, key_cols, key_base = jax.random.split(key, 3)
    row_scale = jnp.exp(jax.random.uniform(key_rows, (FF, 1)) * jnp.log(10.0))
    ramp = jnp.arange(D, dtype=jnp.float32) / D
    col_scale = 10.0 ** (0.8 * ramp + 0.2 * jax.random.uniform(key_cols, (D,)))
    base = jnp.clip(jax.random.normal(key_base, (FF, D)), -5.0, 5.0)
    return (0.3 * base * row_scale * col_scale[None, :]).astype(jnp.bfloat16)


def levels(stream_key, extent, cuts, smallest, high):
    factor_of = 1.0
    for position, shards_of in cuts:
        draws = jax.random.uniform(jax.random.fold_in(jax.random.fold_in(stream_key, 6), position), (shards_of,), jnp.float32, smallest / len(cuts), high / len(cuts))
        factor_of = factor_of * jnp.repeat(jnp.exp(draws), extent[position] // shards_of).reshape((-1,) + (1,) * (len(extent) - 1 - position))
    return factor_of


def centred(own_key, dims, width, reach, shards=(), held_as=jnp.bfloat16):
    entries = jax.random.normal(own_key, dims, jnp.float32) * width
    if len(shards) > 0:
        entries = levels(own_key, dims, shards, -0.22, 0.18) * entries
    return jnp.clip(entries, min=-reach, max=reach).astype(held_as)


def setup_inputs(seed: int = 0) -> dict:
    keys = jax.random.split(jax.random.key(seed), 5)
    return {
        "momentum": centred(keys[0], (FF, D), 1.0, 6.0, ((0, 64), (1, 8))),
        "gradient": draw_gradient(jax.random.fold_in(keys[4], 71), 0),
        "right_factor": centred(keys[2], (N_TP, D // N_TP, RANK), D ** -0.5, 0.0625, ((0, 8), (1, 64))),
        "weight": centred(keys[3], (FF, D), 1.0, 6.0, ((0, 64), (1, 8))),
    }


def reference(momentum, gradient, right_factor, weight):
    buffer = (momentum.astype(jnp.float32) + gradient.astype(jnp.float32)).astype(jnp.bfloat16)
    factor = right_factor.reshape(D, RANK)
    sketch = jnp.dot(buffer.astype(jnp.float32), factor.astype(jnp.float32), preferred_element_type=jnp.float32)
    gram = lax.dot_general(sketch, sketch, (((0,), (0,)), ((), ())), precision=lax.Precision.HIGHEST)
    lower = jnp.linalg.cholesky(gram)
    left = jax.scipy.linalg.solve_triangular(lower, sketch.T, lower=True).T
    left_half = left.astype(jnp.bfloat16)
    projected = lax.dot_general(buffer.astype(jnp.float32), left_half.astype(jnp.float32), (((0,), (0,)), ((), ())), preferred_element_type=jnp.float32)
    norms = jnp.sqrt(lax.optimization_barrier(jnp.sum(projected * projected, axis=0)) + 1e-06)
    factor_new = (projected / norms).astype(jnp.bfloat16).reshape(N_TP, D // N_TP, RANK)
    projected_half = projected.astype(jnp.bfloat16)
    scaled_half = (left / norms).astype(jnp.bfloat16)
    approx = jnp.dot(left_half.astype(jnp.float32), projected_half.T.astype(jnp.float32), preferred_element_type=jnp.float32)
    momentum_new = (buffer.astype(jnp.float32) - 0.05 * approx).astype(jnp.bfloat16)
    update = jnp.dot(scaled_half.astype(jnp.float32), projected_half.T.astype(jnp.float32), preferred_element_type=jnp.float32)
    factor_scale = 0.2 * jnp.sqrt(jnp.float32(FF) * jnp.float32(D) / jnp.float32(RANK))
    weight_new = (weight.astype(jnp.float32) - factor_scale * update).astype(jnp.bfloat16)
    return (momentum_new, factor_new, weight_new)
```

```python
import functools

import jax
import jax.numpy as jnp
from jax import lax
from jax.experimental import pallas as pl
from jax.experimental.pallas import tpu as pltpu
from jax.sharding import PartitionSpec as P

D = 8192
FF = 28672
RANK = 512
NX, NY, NC, NZ = 4, 8, 2, 8
ROWS = FF // (NX * NY * NC)
COLS = D // NZ
SHARE = COLS // (NX * NY * NC)
ZR = ROWS // NZ
MESH = pl.DeviceIdType.MESH
HI = lax.Precision.HIGHEST
F32 = jnp.float32
BF16 = jnp.bfloat16

PHASES = {}
_n = 0
for _name, _k in (
    ("fy", 7), ("fx", 3), ("fc", 4), ("sz", 7), ("sg", 7),
    ("gc", 1), ("gx", 3), ("gy", 7), ("gz", 7), ("hy", 7), ("hx", 3), ("hc", 4),
    ("pc", 1), ("px", 3), ("py", 7), ("qy", 7), ("qx", 3), ("qc", 4), ("nz", 7),
):
    PHASES[_name] = _n
    _n += _k
N_SEMS = _n


def wide(x):
    return jnp.broadcast_to(x, (8, 128))


def diag_inverse(m):
    lane = lax.broadcasted_iota(jnp.int32, (8, 128), 1)
    sub = lax.broadcasted_iota(jnp.int32, (8, 128), 0)
    m = list(m)
    n = len(m)
    out = []
    for k in range(n):
        lo = 8 * k
        v = m[k]
        inside = (lane >= lo) & (lane < lo + 8)
        cols = [wide(v[:, lo + j : lo + j + 1]) for j in range(8)]
        a = [[wide(cols[j][i : i + 1, :]) if j <= i else None for j in range(8)] for i in range(8)]
        vi = jnp.where(inside, jnp.where(lane - lo == sub, 1.0, 0.0), v)
        vb = [wide(vi[j : j + 1, :]) for j in range(8)]
        rs = [None] * 8
        r = [None] * 8
        for j in range(8):
            rs[j] = lax.rsqrt(a[j][j])
            r[j] = vb[j] * rs[j]
            for i in range(j + 1, 8):
                a[i][j] = a[i][j] * rs[j]
            for i in range(j + 1, 8):
                for c in range(j + 1, i + 1):
                    a[i][c] = a[i][c] - a[i][j] * a[c][j]
                vb[i] = vb[i] - a[i][j] * r[j]
        q = [None] * 8
        acc = list(r)
        for j in range(7, -1, -1):
            q[j] = acc[j] * rs[j]
            for i in range(j):
                acc[i] = acc[i] - a[j][i] * q[j]
        row = r[0]
        for j in range(1, 8):
            row = jnp.where(sub == j, r[j], row)
        out.append(row)
        for i in range(k + 1, n):
            base = jnp.where(inside, 0.0, m[i])
            t = [wide(m[i][:, lo + j : lo + j + 1]) * q[j] for j in range(8)]
            s = ((t[0] + t[1]) + (t[2] + t[3])) + ((t[4] + t[5]) + (t[6] + t[7]))
            m[i] = base - s
    return out


def split(x):
    hi = x.astype(BF16)
    return hi, (x - hi.astype(F32)).astype(BF16)


def dot_nt(a, b):
    return lax.dot_general(a, b, (((1,), (1,)), ((), ())), preferred_element_type=F32)


def dot_tn(a, b, precision=None):
    return lax.dot_general(
        a, b, (((0,), (0,)), ((), ())), precision=precision, preferred_element_type=F32
    )


def kernel(
    m_hbm, g_hbm, f_hbm, w_hbm,
    mo_hbm, fo_hbm, wo_hbm,
    m_v, g_v, w_v, b_v, f_v, sk_v, skr_v, so_v, sa_v, sh_v, sl_v,
    gs_v, gm_v, gcr_v, gxr_v, g1_v, gyr_v, gzr_v, gg_v, ch_v, dd_v,
    ps_v, pm_v, pcr_v, pxr_v, p1_v, pyr_v, pf_v,
    xh_v, xl_v, le_v, lh_v, ph_v, nz_v, fo_v,
    send_sem, recv_sem, local_sem,
):
    i = lax.axis_index("fsdp")
    z = lax.axis_index("tp")
    c = lax.rem(i, NC)
    y = lax.rem(i // NC, NY)
    x = i // (NC * NY)

    def at(x_, y_, c_):
        return (x_ * NY + y_) * NC + c_

    def around(v, d, n):
        return lax.rem(v + d, n)

    def remote(phase, k, src, dst, fsdp, tp):
        s = PHASES[phase] + k
        return pltpu.make_async_remote_copy(
            src_ref=src, dst_ref=dst, send_sem=send_sem.at[s], recv_sem=recv_sem.at[s],
            device_id=(fsdp, tp), device_id_type=MESH,
        )

    xs = [around(x, d, NX) for d in range(NX)]
    ys = [around(y, d, NY) for d in range(NY)]
    zs = [around(z, d, NZ) for d in range(NZ)]
    other = at(x, y, 1 - c)

    def to_x(phase, src, dst):
        return [remote(phase, d - 1, src(xs[d], d), dst(xs[d], d), at(xs[d], y, c), z) for d in range(1, NX)]

    def to_y(phase, src, dst):
        return [remote(phase, d - 1, src(ys[d], d), dst(ys[d], d), at(x, ys[d], c), z) for d in range(1, NY)]

    def to_z(phase, src, dst):
        return [remote(phase, d - 1, src(zs[d], d), dst(zs[d], d), i, zs[d]) for d in range(1, NZ)]

    def to_core(phase, src, dst):
        return [remote(phase, 0, src, dst, other, z)]

    def rows(ref, start, size):
        return ref.at[pl.ds(pl.multiple_of(start, 8), size)]

    f_mine = f_v.at[x, :, c]
    fy = to_y("fy", lambda p, d: f_hbm.at[0], lambda p, d: f_v.at[x, y, c])
    fx = to_x("fx", lambda p, d: f_mine, lambda p, d: f_mine)
    fc = [
        remote("fc", d, f_v.at[around(x, NX - d, NX), :, c], f_v.at[around(x, NX - d, NX), :, c], other, z)
        for d in range(NX)
    ]
    sz = to_z("sz", lambda p, d: rows(sk_v, p * ZR, ZR), lambda p, d: skr_v.at[d - 1])
    sg = to_z("sg", lambda p, d: so_v, lambda p, d: rows(sa_v, z * ZR, ZR))
    gc = to_core("gc", gs_v, gcr_v)
    gx = to_x("gx", lambda p, d: rows(gm_v, p * 64, 64), lambda p, d: gxr_v.at[d - 1])
    gy = to_y("gy", lambda p, d: rows(g1_v, p * 8, 8), lambda p, d: gyr_v.at[d - 1])
    gz = to_z("gz", lambda p, d: gzr_v.at[z], lambda p, d: gzr_v.at[z])
    g_y = rows(gg_v, c * 256 + x * 64 + y * 8, 8)
    hy = to_y("hy", lambda p, d: g_y, lambda p, d: g_y)
    g_x = rows(gg_v, c * 256 + x * 64, 64)
    hx = to_x("hx", lambda p, d: g_x, lambda p, d: g_x)
    hc = []
    for d in range(NX):
        piece = rows(gg_v, c * 256 + around(x, NX - d, NX) * 64, 64)
        hc.append(remote("hc", d, piece, piece, other, z))
    pc = to_core("pc", ps_v, pcr_v)
    px = to_x("px", lambda p, d: rows(pm_v, p * 128, 128), lambda p, d: pxr_v.at[d - 1])
    py = to_y("py", lambda p, d: rows(p1_v, p * 16, 16), lambda p, d: pyr_v.at[d - 1])
    p_y = rows(pf_v, c * 512 + x * 128 + y * 16, 16)
    qy = to_y("qy", lambda p, d: p_y, lambda p, d: p_y)
    p_x = rows(pf_v, c * 512 + x * 128, 128)
    qx = to_x("qx", lambda p, d: p_x, lambda p, d: p_x)
    qc = []
    for d in range(NX):
        piece = rows(pf_v, c * 512 + around(x, NX - d, NX) * 128, 128)
        qc.append(remote("qc", d, piece, piece, other, z))
    nz = to_z("nz", lambda p, d: nz_v.at[z], lambda p, d: nz_v.at[z])

    def start(copies):
        for k in copies:
            k.start()

    def landed(copies):
        for k in copies:
            k.wait_recv()

    load_m = pltpu.make_async_copy(m_hbm, m_v, local_sem.at[0])
    load_g = pltpu.make_async_copy(g_hbm, g_v, local_sem.at[1])
    load_f = pltpu.make_async_copy(f_hbm.at[0], f_v.at[x, y, c], local_sem.at[2])
    load_w = pltpu.make_async_copy(w_hbm, w_v, local_sem.at[3])
    load_f.start()
    load_m.start()
    load_g.start()
    load_w.start()

    barrier = pltpu.get_barrier_semaphore()
    peers = (
        [(at(xs[d], y, c), z) for d in range(1, NX)]
        + [(at(x, ys[d], c), z) for d in range(1, NY)]
        + [(i, zs[d]) for d in range(1, NZ)]
        + [(other, z)]
    )
    for peer in peers:
        pl.semaphore_signal(barrier, inc=1, device_id=peer, device_id_type=MESH)
    pl.semaphore_wait(barrier, len(peers))

    start(fy)
    load_m.wait()
    load_g.wait()

    def add_buffer(k, _):
        r = pl.ds(pl.multiple_of(k * 64, 64), 64)
        b_v[r, :] = (m_v[r, :].astype(F32) + g_v[r, :].astype(F32)).astype(BF16)
        return 0

    lax.fori_loop(0, ROWS // 64, add_buffer, 0)
    load_f.wait()
    landed(fy)
    start(fx)
    fc[0].start()
    for d in range(1, NX):
        fx[d - 1].wait_recv()
        fc[d].start()
    landed(fc)

    def sketch_rows(k, _):
        r = pl.ds(pl.multiple_of(k * 64, 64), 64)
        sk_v[r, :] = jnp.dot(b_v[r, :], f_v[...].reshape(COLS, RANK), preferred_element_type=F32)
        return 0

    lax.fori_loop(0, ROWS // 64, sketch_rows, 0)
    start(sz)
    total = sk_v[pl.ds(pl.multiple_of(z * ZR, 8), ZR), :]
    for d in range(1, NZ):
        sz[d - 1].wait_recv()
        total = total + skr_v[d - 1]
    so_v[...] = total
    start(sg)
    sa_v[pl.ds(pl.multiple_of(z * ZR, 8), ZR), :] = total

    far = pl.ds(pl.multiple_of((1 - c) * 256, 256), 256)
    near = pl.ds(pl.multiple_of(c * 256, 256), 256)
    gs_v[...] = dot_tn(so_v[:, far], so_v[...], HI)
    start(gc)
    gm_v[...] = dot_tn(so_v[:, near], so_v[...], HI)
    landed(gc)
    gm_v[...] = gm_v[...] + gcr_v[...]
    start(gx)
    total = gm_v[pl.ds(pl.multiple_of(x * 64, 64), 64), :]
    for d in range(1, NX):
        gx[d - 1].wait_recv()
        total = total + gxr_v[d - 1]
    g1_v[...] = total
    start(gy)
    total = g1_v[pl.ds(pl.multiple_of(y * 8, 8), 8), :]
    for d in range(1, NY):
        gy[d - 1].wait_recv()
        total = total + gyr_v[d - 1]
    gzr_v[z] = total
    start(gz)

    landed(sg)

    def split_rows(k, _):
        r = pl.ds(pl.multiple_of(k * 64, 64), 64)
        hi, lo = split(sa_v[r, :])
        sh_v[r, :] = hi
        sl_v[r, :] = lo
        return 0

    lax.fori_loop(0, ROWS // 64, split_rows, 0)

    def project(half, out):
        def tile(k, _):
            cols = pl.ds(pl.multiple_of(half * 512 + k * 128, 128), 128)
            out[pl.ds(pl.multiple_of(k * 128, 128), 128), :] = dot_tn(b_v[:, cols], sh_v[...]) + dot_tn(
                b_v[:, cols], sl_v[...]
            )
            return 0

        lax.fori_loop(0, 4, tile, 0)

    project(1 - c, ps_v)
    start(pc)
    landed(gz)
    total = gzr_v[0]
    for d in range(1, NZ):
        total = total + gzr_v[d]
    gg_v[pl.ds(pl.multiple_of(c * 256 + x * 64 + y * 8, 8), 8), :] = total
    start(hy)
    project(c, pm_v)
    landed(hy)
    start(hx)
    hc[0].start()
    for d in range(1, NX):
        hx[d - 1].wait_recv()
        hc[d].start()

    landed(pc)

    def add_half(k, _):
        r = pl.ds(pl.multiple_of(k * 64, 64), 64)
        pm_v[r, :] = pm_v[r, :] + pcr_v[r, :]
        return 0

    lax.fori_loop(0, 8, add_half, 0)
    start(px)
    landed(hc)

    def progress(step):
        if step == 0:
            total = pm_v[pl.ds(pl.multiple_of(x * 128, 128), 128), :]
            for d in range(1, NX):
                px[d - 1].wait_recv()
                total = total + pxr_v[d - 1]
            p1_v[...] = total
            start(py)
        elif step == 1:
            total = p1_v[pl.ds(pl.multiple_of(y * 16, 16), 16), :]
            for d in range(1, NY):
                py[d - 1].wait_recv()
                total = total + pyr_v[d - 1]
            pf_v[pl.ds(pl.multiple_of(c * 512 + x * 128 + y * 16, 16), 16), :] = total
            start(qy)
        elif step == 2:
            landed(qy)
            start(qx)
            qc[0].start()
        elif step == 3:
            for d in range(1, NX):
                qx[d - 1].wait_recv()
                qc[d].start()

    nb = RANK // 128

    def copy_gram(k, _):
        r = pl.ds(pl.multiple_of(k * 64, 64), 64)
        ch_v[r, :] = gg_v[r, :]
        return 0

    lax.fori_loop(0, 8, copy_gram, 0)

    def eliminate(k, _):
        off = pl.multiple_of(k * 128, 128)
        mine = pl.ds(off, 128)
        blk = ch_v[mine, mine]
        done = diag_inverse([blk[8 * j : 8 * j + 8, :] for j in range(16)])
        for j in range(16):
            dd_v[8 * j : 8 * j + 8, :] = done[j]
        for step in range(4):
            @pl.when(k == step)
            def _():
                progress(step)
        r128 = lax.broadcasted_iota(jnp.int32, (128, 128), 0)
        c128 = lax.broadcasted_iota(jnp.int32, (128, 128), 1)
        linv = jnp.where(r128 >= c128, dd_v[...], 0.0)
        ch_v[mine, mine] = jnp.where(r128 == c128, 1.0, 0.0)
        r = jnp.dot(linv, ch_v[mine, :], precision=HI, preferred_element_type=F32)
        ch_v[mine, :] = r

        def update(k2, _):
            theirs = pl.ds(pl.multiple_of(k2 * 128, 128), 128)
            u = ch_v[mine, theirs]
            ch_v[theirs, mine] = jnp.zeros((128, 128), F32)
            ch_v[theirs, :] = ch_v[theirs, :] - dot_tn(u, r, HI)
            return 0

        lax.fori_loop(k + 1, nb, update, 0)
        return 0

    lax.fori_loop(0, nb, eliminate, 0)

    def split_inverse(k, _):
        r = pl.ds(pl.multiple_of(k * 64, 64), 64)
        rr = lax.broadcasted_iota(jnp.int32, (64, RANK), 0) + k * 64
        cc = lax.broadcasted_iota(jnp.int32, (64, RANK), 1)
        hi, lo = split(jnp.where(rr >= cc, ch_v[r, :], 0.0))
        xh_v[r, :] = hi
        xl_v[r, :] = lo
        return 0

    lax.fori_loop(0, 8, split_inverse, 0)

    landed(qc)
    for copies in (qy, qx, qc):
        for k in copies:
            k.wait_send()
    nz_v[z] = jnp.zeros((8, RANK), F32)

    def projected_rows(k, _):
        r = pl.ds(pl.multiple_of(k * 128, 128), 128)
        hi, lo = split(pf_v[r, :])
        p = dot_nt(hi, xh_v[...]) + (dot_nt(hi, xl_v[...]) + dot_nt(lo, xh_v[...]))
        pf_v[r, :] = p
        ph_v[r, :] = p.astype(BF16)
        nz_v[z] = nz_v[z] + jnp.sum((p * p).reshape(16, 8, RANK), axis=0)
        return 0

    lax.fori_loop(0, COLS // 128, projected_rows, 0)
    start(nz)

    def left_rows(k, _):
        r = pl.ds(pl.multiple_of(k * 64, 64), 64)
        hi, lo = sh_v[r, :], sl_v[r, :]
        left = dot_nt(hi, xh_v[...]) + (dot_nt(hi, xl_v[...]) + dot_nt(lo, xh_v[...]))
        le_v[r, :] = left
        lh_v[r, :] = left.astype(BF16)
        return 0

    lax.fori_loop(0, ROWS // 64, left_rows, 0)

    def momentum_rows(k, _):
        r = pl.ds(pl.multiple_of(k * 64, 64), 64)
        approx = dot_nt(lh_v[r, :], ph_v[...])
        m_v[r, :] = (b_v[r, :].astype(F32) - 0.05 * approx).astype(BF16)
        return 0

    lax.fori_loop(0, ROWS // 64, momentum_rows, 0)
    store_m = pltpu.make_async_copy(m_v, mo_hbm, local_sem.at[0])
    store_m.start()

    landed(nz)
    total = nz_v[0]
    for d in range(1, NZ):
        total = total + nz_v[d]
    inv = 1.0 / jnp.sqrt(jnp.sum(total, axis=0, keepdims=True) + 1e-06)
    fo_v[0] = (pf_v[pl.ds(pl.multiple_of(i * SHARE, SHARE), SHARE), :] * inv).astype(BF16)
    store_f = pltpu.make_async_copy(fo_v, fo_hbm, local_sem.at[2])
    store_f.start()
    load_w.wait()
    scale = 0.2 * (FF * D / RANK) ** 0.5

    def weight_rows(k, _):
        r = pl.ds(pl.multiple_of(k * 64, 64), 64)
        scaled = (le_v[r, :] * inv).astype(BF16)
        w_v[r, :] = (w_v[r, :].astype(F32) - scale * dot_nt(scaled, ph_v[...])).astype(BF16)
        return 0

    lax.fori_loop(0, ROWS // 64, weight_rows, 0)
    store_w = pltpu.make_async_copy(w_v, wo_hbm, local_sem.at[3])
    store_w.start()

    for copies in (fy, fx, fc, sz, sg, gc, gx, gy, gz, hy, hx, hc, pc, px, py, nz):
        for k in copies:
            k.wait_send()
    store_m.wait()
    store_f.wait()
    store_w.wait()


def local(momentum, gradient, right_factor, weight):
    any_spec = pl.BlockSpec(memory_space=pl.ANY)
    v = pltpu.VMEM
    return pl.pallas_call(
        kernel,
        out_shape=(
            jax.ShapeDtypeStruct((ROWS, COLS), BF16),
            jax.ShapeDtypeStruct((1, SHARE, RANK), BF16),
            jax.ShapeDtypeStruct((ROWS, COLS), BF16),
        ),
        in_specs=[any_spec] * 4,
        out_specs=(any_spec,) * 3,
        scratch_shapes=[
            v((ROWS, COLS), BF16), v((ROWS, COLS), BF16), v((ROWS, COLS), BF16), v((ROWS, COLS), BF16),
            v((NX, NY, NC, SHARE, RANK), BF16),
            v((ROWS, RANK), F32), v((7, ZR, RANK), F32), v((ZR, RANK), F32), v((ROWS, RANK), F32),
            v((ROWS, RANK), BF16), v((ROWS, RANK), BF16),
            v((256, RANK), F32), v((256, RANK), F32), v((256, RANK), F32),
            v((3, 64, RANK), F32), v((64, RANK), F32), v((7, 8, RANK), F32), v((8, 8, RANK), F32),
            v((RANK, RANK), F32), v((RANK, RANK), F32), v((128, 128), F32),
            v((512, RANK), F32), v((512, RANK), F32), v((512, RANK), F32),
            v((3, 128, RANK), F32), v((128, RANK), F32), v((7, 16, RANK), F32), v((COLS, RANK), F32),
            v((RANK, RANK), BF16), v((RANK, RANK), BF16),
            v((ROWS, RANK), F32), v((ROWS, RANK), BF16), v((COLS, RANK), BF16),
            v((8, 8, RANK), F32), v((1, SHARE, RANK), BF16),
            pltpu.SemaphoreType.DMA((N_SEMS,)),
            pltpu.SemaphoreType.DMA((N_SEMS,)),
            pltpu.SemaphoreType.DMA((4,)),
        ],
        compiler_params=pltpu.CompilerParams(
            collective_id=0, has_side_effects=True, vmem_limit_bytes=48 * 2**20
        ),
        name="dion_step",
    )(momentum, gradient, right_factor, weight)


def solution(mesh):
    return jax.shard_map(
        local,
        mesh=mesh,
        in_specs=(P("fsdp", "tp"), P("fsdp", "tp"), P("tp", "fsdp", None), P("fsdp", "tp")),
        out_specs=(P("fsdp", "tp"), P("tp", "fsdp", None), P("fsdp", "tp")),
        check_vma=False,
    )
```

```python
import functools

import jax
import jax.numpy as jnp
from jax import lax
from jax.experimental import pallas as pl
from jax.experimental.pallas import tpu as pltpu
from jax.sharding import PartitionSpec as P

D = 8192
FF = 28672
RANK = 512
NX, NY, NC, NZ = 4, 8, 2, 8
ROWS = FF // (NX * NY * NC)
COLS = D // NZ
SHARE = COLS // (NX * NY * NC)
ZR = ROWS // NZ
MESH = pl.DeviceIdType.MESH
HI = lax.Precision.HIGHEST
F32 = jnp.float32
BF16 = jnp.bfloat16

PHASES = {}
_n = 0
for _name, _k in (
    ("fy", 7), ("fx", 6), ("fc", 4), ("sz", 14), ("sg", 7),
    ("gc", 1), ("gx", 6), ("gy", 7), ("gz", 7), ("hy", 7), ("hx", 6), ("hc", 4),
    ("pc", 1), ("px", 6), ("py", 7), ("qy", 7), ("qx", 6), ("qc", 4), ("nz", 7),
):
    PHASES[_name] = _n
    _n += _k
N_SEMS = _n


def wide(x):
    return jnp.broadcast_to(x, (8, 128))


def diag_inverse(m, between):
    lane = lax.broadcasted_iota(jnp.int32, (8, 128), 1)
    sub = lax.broadcasted_iota(jnp.int32, (8, 128), 0)

    def pick(rows):
        row = rows[0]
        for j in range(1, 8):
            row = jnp.where(sub == j, rows[j], row)
        return row

    m = list(m)
    n = len(m)
    out = []
    for k in range(n):
        between(k)
        lo = 8 * k
        v = m[k]
        inside = (lane >= lo) & (lane < lo + 8)
        cols = [wide(v[:, lo + j : lo + j + 1]) for j in range(8)]
        a = [[wide(cols[j][i : i + 1, :]) if j <= i else None for j in range(8)] for i in range(8)]
        vi = jnp.where(inside, jnp.where(lane - lo == sub, 1.0, 0.0), v)
        vb = [wide(vi[j : j + 1, :]) for j in range(8)]
        near = range(k + 1, min(n, k + 3))
        far = k + 3
        nx = [[wide(m[b][:, lo + j : lo + j + 1]) for j in range(8)] for b in near]
        nl = [[None] * 8 for _ in near]
        new = [jnp.where(inside, 0.0, m[b]) for b in near]
        rs = [None] * 8
        r = [None] * 8
        for j in range(8):
            rs[j] = lax.rsqrt(a[j][j])
            r[j] = vb[j] * rs[j]
            for b in range(len(near)):
                nl[b][j] = nx[b][j] * rs[j]
            for i in range(j + 1, 8):
                a[i][j] = a[i][j] * rs[j]
            for i in range(j + 1, 8):
                for c in range(j + 1, i + 1):
                    a[i][c] = a[i][c] - a[i][j] * a[c][j]
                vb[i] = vb[i] - a[i][j] * r[j]
                for b in range(len(near)):
                    nx[b][i] = nx[b][i] - a[i][j] * nl[b][j]
            for b in range(len(near)):
                new[b] = new[b] - nl[b][j] * r[j]
        out.append(pick(r))
        if far < n:
            q = [None] * 8
            acc = list(r)
            for j in range(7, -1, -1):
                q[j] = acc[j] * rs[j]
                for i in range(j):
                    acc[i] = acc[i] - a[j][i] * q[j]
            padded = [jnp.zeros((8, 128), F32)] * n
            padded[k] = pick(q)
            t = jnp.dot(
                jnp.concatenate(m[far:], axis=0), jnp.concatenate(padded, axis=0),
                precision=HI, preferred_element_type=F32,
            )
            for i in range(far, n):
                m[i] = jnp.where(inside, 0.0, m[i]) - t[8 * (i - far) : 8 * (i - far) + 8, :]
        for b, i in enumerate(near):
            m[i] = new[b]
    return out


def split(x):
    hi = x.astype(BF16)
    return hi, (x - hi.astype(F32)).astype(BF16)


def dot_nt(a, b):
    return lax.dot_general(a, b, (((1,), (1,)), ((), ())), preferred_element_type=F32)


def dot_tn(a, b, precision=None):
    return lax.dot_general(
        a, b, (((0,), (0,)), ((), ())), precision=precision, preferred_element_type=F32
    )


def kernel(
    m_hbm, g_hbm, f_hbm, w_hbm,
    mo_hbm, fo_hbm, wo_hbm,
    m_v, g_v, w_v, b_v, f_v, sk_v, up_v, dn_v, so_v, sa_v, sh_v, sl_v,
    gs_v, gm_v, gcr_v, gxr_v, g1_v, gyr_v, gzr_v, gg_v, ch_v,
    ps_v, pm_v, pcr_v, pxr_v, p1_v, pyr_v, pf_v,
    xh_v, xl_v, le_v, lh_v, ph_v, nz_v, fo_v,
    send_sem, recv_sem, local_sem,
):
    i = lax.axis_index("fsdp")
    z = lax.axis_index("tp")
    c = lax.rem(i, NC)
    y = lax.rem(i // NC, NY)
    x = i // (NC * NY)

    def at(x_, y_, c_):
        return (x_ * NY + y_) * NC + c_

    def around(v, d, n):
        return lax.rem(v + d, n)

    def remote(phase, k, src, dst, fsdp, tp):
        s = PHASES[phase] + k
        return pltpu.make_async_remote_copy(
            src_ref=src, dst_ref=dst, send_sem=send_sem.at[s], recv_sem=recv_sem.at[s],
            device_id=(fsdp, tp), device_id_type=MESH,
        )

    xs = [around(x, d, NX) for d in range(NX)]
    ys = [around(y, d, NY) for d in range(NY)]
    zs = [around(z, d, NZ) for d in range(NZ)]
    other = at(x, y, 1 - c)

    def to_y(phase, src, dst):
        return [remote(phase, d - 1, src(ys[d], d), dst(ys[d], d), at(x, ys[d], c), z) for d in range(1, NY)]

    def to_z(phase, src, dst):
        return [remote(phase, d - 1, src(zs[d], d), dst(zs[d], d), i, zs[d]) for d in range(1, NZ)]

    def to_core(phase, src, dst):
        return [remote(phase, 0, src, dst, other, z)]

    def rows(ref, start, size):
        return ref.at[pl.ds(pl.multiple_of(start, 8), size)]

    def x_sums(phase, src, size, slots):
        half = size // 2

        def a(p):
            return rows(src, p * size, half)

        def b(p):
            return rows(src, p * size + half, half)

        right, left = at(xs[1], y, c), at(xs[3], y, c)
        return [
            remote(phase, 0, a(xs[2]), slots.at[0], right, z),
            remote(phase, 1, b(xs[2]), slots.at[1], left, z),
            remote(phase, 2, b(xs[1]), slots.at[2], right, z),
            remote(phase, 3, a(xs[3]), slots.at[3], left, z),
            remote(phase, 4, slots.at[0], slots.at[4], right, z),
            remote(phase, 5, slots.at[1], slots.at[5], left, z),
        ]

    def x_sums_forward(copies, src, size, slots):
        half = size // 2
        copies[0].wait_recv()
        slots[0] = slots[0] + src[pl.ds(pl.multiple_of(xs[1] * size, 8), half), :]
        copies[4].start()
        copies[1].wait_recv()
        slots[1] = slots[1] + src[pl.ds(pl.multiple_of(xs[3] * size + half, 8), half), :]
        copies[5].start()

    def x_sums_finish(copies, src, size, slots, out):
        half = size // 2
        for k in (2, 3, 4, 5):
            copies[k].wait_recv()
        out[0:half, :] = src[pl.ds(pl.multiple_of(x * size, 8), half), :] + (slots[3] + slots[4])
        out[half:size, :] = src[pl.ds(pl.multiple_of(x * size + half, 8), half), :] + (slots[2] + slots[5])

    def x_all(phase, a, b):
        right, left = at(xs[1], y, c), at(xs[3], y, c)
        return [
            remote(phase, 0, a(x), a(x), right, z),
            remote(phase, 1, b(x), b(x), left, z),
            remote(phase, 2, b(x), b(x), right, z),
            remote(phase, 3, a(x), a(x), left, z),
            remote(phase, 4, a(xs[3]), a(xs[3]), right, z),
            remote(phase, 5, b(xs[1]), b(xs[1]), left, z),
        ]

    def x_all_forward(copies):
        copies[0].wait_recv()
        copies[4].start()
        copies[1].wait_recv()
        copies[5].start()

    def x_all_finish(copies, across):
        copies[2].wait_recv()
        across[0].start()
        copies[3].wait_recv()
        across[1].start()
        copies[4].wait_recv()
        copies[5].wait_recv()
        across[2].start()

    def f_half(h):
        return lambda p: f_v.at[p, pl.ds(h * (NY // 2), NY // 2), c]

    def g_half(h):
        return lambda p: rows(gg_v, c * 256 + p * 64 + h * 32, 32)

    def p_half(h):
        return lambda p: rows(pf_v, c * 512 + p * 128 + h * 64, 64)

    def across(phase, block):
        return [remote(phase, k, block(xs[d]), block(xs[d]), other, z) for k, d in enumerate((0, 3, 1, 2))]

    fy = to_y("fy", lambda p, d: f_hbm.at[0], lambda p, d: f_v.at[x, y, c])
    fx = x_all("fx", f_half(0), f_half(1))
    fc = across("fc", lambda p: f_v.at[p, :, c])

    parts = ((0, 24), (24, 32))
    up, down = [], []
    for s in range(4):
        for h, (first, size) in enumerate(parts):
            src = rows(sk_v, zs[4] * ZR + first, size) if s == 0 else up_v.at[s - 1, pl.ds(first, size)]
            up.append(remote("sz", 2 * s + h, src, up_v.at[s, pl.ds(first, size)], i, zs[1]))
    for s in range(3):
        for h, (first, size) in enumerate(parts):
            src = rows(sk_v, zs[5] * ZR + first, size) if s == 0 else dn_v.at[s - 1, pl.ds(first, size)]
            down.append(remote("sz", 8 + 2 * s + h, src, dn_v.at[s, pl.ds(first, size)], i, zs[7]))
    sg_up = []
    for s in range(4):
        piece = rows(sa_v, zs[(8 - s) % 8] * ZR, ZR)
        sg_up.append(remote("sg", s, so_v if s == 0 else piece, piece, i, zs[1]))
    sg_down = []
    for s in range(3):
        piece = rows(sa_v, zs[s] * ZR, ZR)
        sg_down.append(remote("sg", 4 + s, so_v if s == 0 else piece, piece, i, zs[7]))

    gc = to_core("gc", gs_v, gcr_v)
    gx = x_sums("gx", gm_v, 64, gxr_v)
    gy = to_y("gy", lambda p, d: rows(g1_v, p * 8, 8), lambda p, d: gyr_v.at[d - 1])
    gz = to_z("gz", lambda p, d: gzr_v.at[z], lambda p, d: gzr_v.at[z])
    g_y = rows(gg_v, c * 256 + x * 64 + y * 8, 8)
    hy = to_y("hy", lambda p, d: g_y, lambda p, d: g_y)
    hx = x_all("hx", g_half(0), g_half(1))
    hc = across("hc", lambda p: rows(gg_v, c * 256 + p * 64, 64))
    pc = to_core("pc", ps_v, pcr_v)
    px = x_sums("px", pm_v, 128, pxr_v)
    py = to_y("py", lambda p, d: rows(p1_v, p * 16, 16), lambda p, d: pyr_v.at[d - 1])
    p_y = rows(pf_v, c * 512 + x * 128 + y * 16, 16)
    qy = to_y("qy", lambda p, d: p_y, lambda p, d: p_y)
    qx = x_all("qx", p_half(0), p_half(1))
    qc = across("qc", lambda p: rows(pf_v, c * 512 + p * 128, 128))
    nz = to_z("nz", lambda p, d: nz_v.at[z], lambda p, d: nz_v.at[z])

    def start(copies):
        for k in copies:
            k.start()

    def landed(copies):
        for k in copies:
            k.wait_recv()

    load_m = pltpu.make_async_copy(m_hbm, m_v, local_sem.at[0])
    load_g = pltpu.make_async_copy(g_hbm, g_v, local_sem.at[1])
    load_f = pltpu.make_async_copy(f_hbm.at[0], f_v.at[x, y, c], local_sem.at[2])
    load_w = pltpu.make_async_copy(w_hbm, w_v, local_sem.at[3])
    load_f.start()
    load_m.start()
    load_g.start()
    load_w.start()

    barrier = pltpu.get_barrier_semaphore()
    peers = (
        [(at(xs[d], y, c), z) for d in (1, 3)]
        + [(at(x, ys[d], c), z) for d in range(1, NY)]
        + [(i, zs[d]) for d in range(1, NZ)]
        + [(other, z)]
    )
    for peer in peers:
        pl.semaphore_signal(barrier, inc=1, device_id=peer, device_id_type=MESH)
    pl.semaphore_wait(barrier, len(peers))

    start(fy)
    load_m.wait()
    load_g.wait()

    def add_buffer(k, _):
        r = pl.ds(pl.multiple_of(k * 64, 64), 64)
        b_v[r, :] = (m_v[r, :].astype(F32) + g_v[r, :].astype(F32)).astype(BF16)
        return 0

    lax.fori_loop(0, ROWS // 64, add_buffer, 0)
    load_f.wait()
    landed(fy)
    start(fx[:4])
    fc[0].start()
    x_all_forward(fx)
    x_all_finish(fx, fc[1:])
    landed(fc)

    sk_v[...] = jnp.dot(b_v[...], f_v[...].reshape(COLS, RANK), preferred_element_type=F32)
    start(up[:2])
    start(down[:2])
    for s in range(1, 4):
        for h, (first, size) in enumerate(parts):
            part = pl.ds(first, size)
            up[2 * s - 2 + h].wait_recv()
            mine = pl.ds(pl.multiple_of(zs[4 - s] * ZR + first, 8), size)
            up_v[s - 1, part, :] = up_v[s - 1, part, :] + sk_v[mine, :]
            up[2 * s + h].start()
            if s < 3:
                down[2 * s - 2 + h].wait_recv()
                mine = pl.ds(pl.multiple_of(zs[5 + s] * ZR + first, 8), size)
                dn_v[s - 1, part, :] = dn_v[s - 1, part, :] + sk_v[mine, :]
                down[2 * s + h].start()
    landed(down[4:])
    landed(up[6:])
    total = sk_v[pl.ds(pl.multiple_of(z * ZR, 8), ZR), :] + (up_v[3] + dn_v[2])
    so_v[...] = total
    sg_up[0].start()
    sg_down[0].start()
    sa_v[pl.ds(pl.multiple_of(z * ZR, 8), ZR), :] = total

    def sg_forward(s):
        sg_up[s - 1].wait_recv()
        sg_up[s].start()
        if s < 3:
            sg_down[s - 1].wait_recv()
            sg_down[s].start()

    far = pl.ds(pl.multiple_of((1 - c) * 256, 256), 256)
    near = pl.ds(pl.multiple_of(c * 256, 256), 256)
    gs_v[...] = dot_tn(so_v[:, far], so_v[...], HI)
    start(gc)
    gm_v[...] = dot_tn(so_v[:, near], so_v[...], HI)
    landed(gc)
    gm_v[...] = gm_v[...] + gcr_v[...]
    start(gx[:4])
    sg_forward(1)
    x_sums_forward(gx, gm_v, 64, gxr_v)
    sg_forward(2)
    x_sums_finish(gx, gm_v, 64, gxr_v, g1_v)
    start(gy)
    sg_forward(3)
    total = g1_v[pl.ds(pl.multiple_of(y * 8, 8), 8), :]
    for d in range(1, NY):
        gy[d - 1].wait_recv()
        total = total + gyr_v[d - 1]
    gzr_v[z] = total
    start(gz)

    landed(sg_up[3:])
    landed(sg_down[2:])
    sh_v[...], sl_v[...] = split(sa_v[...])

    def project(half):
        cols = pl.ds(pl.multiple_of(half * 512, 512), 512)
        return dot_tn(b_v[:, cols], sh_v[...]) + dot_tn(b_v[:, cols], sl_v[...])

    ps_v[...] = project(1 - c)
    start(pc)
    landed(gz)
    total = gzr_v[0]
    for d in range(1, NZ):
        total = total + gzr_v[d]
    gg_v[pl.ds(pl.multiple_of(c * 256 + x * 64 + y * 8, 8), 8), :] = total
    start(hy)
    pm_v[...] = project(c)
    landed(hy)
    start(hx[:4])
    hc[0].start()
    landed(pc)
    pm_v[...] = pm_v[...] + pcr_v[...]
    x_all_forward(hx)
    start(px[:4])
    x_all_finish(hx, hc[1:])
    landed(hc)
    x_sums_forward(px, pm_v, 128, pxr_v)

    def progress(step):
        if step == 0:
            x_sums_finish(px, pm_v, 128, pxr_v, p1_v)
            start(py)
        elif step == 1:
            total = p1_v[pl.ds(pl.multiple_of(y * 16, 16), 16), :]
            for d in range(1, NY):
                py[d - 1].wait_recv()
                total = total + pyr_v[d - 1]
            pf_v[pl.ds(pl.multiple_of(c * 512 + x * 128 + y * 16, 16), 16), :] = total
            start(qy)
        elif step == 2:
            landed(qy)
            start(qx[:4])
            qc[0].start()
        elif step == 3:
            x_all_forward(qx)
        elif step == 4:
            x_all_finish(qx, qc[1:])

    nb = RANK // 128

    ch_v[...] = gg_v[...]
    r128 = lax.broadcasted_iota(jnp.int32, (128, 128), 0)
    c128 = lax.broadcasted_iota(jnp.int32, (128, 128), 1)

    def eliminate(k, _):
        mine = pl.ds(pl.multiple_of(k * 128, 128), 128)
        blk = ch_v[mine, mine]

        def between(j):
            for step, (outer, pivot) in enumerate(((0, 5), (1, 5), (2, 5), (2, 11), (3, 8))):
                if j == pivot:

                    @pl.when(k == outer)
                    def _():
                        progress(step)

        done = diag_inverse([blk[8 * j : 8 * j + 8, :] for j in range(16)], between)
        linv = jnp.where(r128 >= c128, jnp.concatenate(done, axis=0), 0.0)
        ch_v[mine, mine] = jnp.where(r128 == c128, 1.0, 0.0)
        ch_v[mine, :] = jnp.dot(linv, ch_v[mine, :], precision=HI, preferred_element_type=F32)
        for kk in range(nb - 1):

            @pl.when(k == kk)
            def _():
                lo, hi = 128 * kk, 128 * (kk + 1)
                ch_v[hi:, lo:hi] = jnp.zeros((RANK - hi, 128), F32)
                ch_v[hi:, :] = ch_v[hi:, :] - dot_tn(ch_v[lo:hi, hi:], ch_v[lo:hi, :], HI)

        return 0

    lax.fori_loop(0, nb, eliminate, 0)
    rr = lax.broadcasted_iota(jnp.int32, (RANK, RANK), 0)
    cc = lax.broadcasted_iota(jnp.int32, (RANK, RANK), 1)
    xh_v[...], xl_v[...] = split(jnp.where(rr >= cc, ch_v[...], 0.0))

    landed(qc)
    for copies in (qy, qx, qc):
        for k in copies:
            k.wait_send()

    def times_inverse(hi, lo):
        return dot_nt(hi, xh_v[...]) + (dot_nt(hi, xl_v[...]) + dot_nt(lo, xh_v[...]))

    proj = times_inverse(*split(pf_v[...]))
    pf_v[...] = proj
    ph_v[...] = proj.astype(BF16)
    nz_v[z] = jnp.sum((proj * proj).reshape(COLS // 8, 8, RANK), axis=0)
    start(nz)

    left = times_inverse(sh_v[...], sl_v[...])
    le_v[...] = left
    lh_v[...] = left.astype(BF16)

    stores = []
    for h in range(2):
        cols = slice(512 * h, 512 * h + 512)
        approx = dot_nt(lh_v[...], ph_v[cols, :])
        m_v[:, cols] = (b_v[:, cols].astype(F32) - 0.05 * approx).astype(BF16)
        stores.append(pltpu.make_async_copy(m_v.at[:, cols], mo_hbm.at[:, cols], local_sem.at[4 + h]))
        stores[-1].start()

    landed(nz)
    total = nz_v[0]
    for d in range(1, NZ):
        total = total + nz_v[d]
    inv = 1.0 / jnp.sqrt(jnp.sum(total, axis=0, keepdims=True) + 1e-06)
    fo_v[0] = (pf_v[pl.ds(pl.multiple_of(i * SHARE, SHARE), SHARE), :] * inv).astype(BF16)
    store_f = pltpu.make_async_copy(fo_v, fo_hbm, local_sem.at[2])
    store_f.start()
    load_w.wait()
    scale = 0.2 * (FF * D / RANK) ** 0.5

    scaled = (le_v[...] * inv).astype(BF16)
    for h in range(2):
        cols = slice(512 * h, 512 * h + 512)
        update = dot_nt(scaled, ph_v[cols, :])
        w_v[:, cols] = (w_v[:, cols].astype(F32) - scale * update).astype(BF16)
        stores.append(pltpu.make_async_copy(w_v.at[:, cols], wo_hbm.at[:, cols], local_sem.at[6 + h]))
        stores[-1].start()

    for copies in (fy, fx, fc, up, down, sg_up, sg_down, gc, gx, gy, gz, hy, hx, hc, pc, px, py, nz):
        for k in copies:
            k.wait_send()
    store_f.wait()
    for store in stores:
        store.wait()


def local(momentum, gradient, right_factor, weight):
    any_spec = pl.BlockSpec(memory_space=pl.ANY)
    v = pltpu.VMEM
    return pl.pallas_call(
        kernel,
        out_shape=(
            jax.ShapeDtypeStruct((ROWS, COLS), BF16),
            jax.ShapeDtypeStruct((1, SHARE, RANK), BF16),
            jax.ShapeDtypeStruct((ROWS, COLS), BF16),
        ),
        in_specs=[any_spec] * 4,
        out_specs=(any_spec,) * 3,
        scratch_shapes=[
            v((ROWS, COLS), BF16), v((ROWS, COLS), BF16), v((ROWS, COLS), BF16), v((ROWS, COLS), BF16),
            v((NX, NY, NC, SHARE, RANK), BF16),
            v((ROWS, RANK), F32), v((4, ZR, RANK), F32), v((3, ZR, RANK), F32), v((ZR, RANK), F32), v((ROWS, RANK), F32),
            v((ROWS, RANK), BF16), v((ROWS, RANK), BF16),
            v((256, RANK), F32), v((256, RANK), F32), v((256, RANK), F32),
            v((6, 32, RANK), F32), v((64, RANK), F32), v((7, 8, RANK), F32), v((8, 8, RANK), F32),
            v((RANK, RANK), F32), v((RANK, RANK), F32),
            v((512, RANK), F32), v((512, RANK), F32), v((512, RANK), F32),
            v((6, 64, RANK), F32), v((128, RANK), F32), v((7, 16, RANK), F32), v((COLS, RANK), F32),
            v((RANK, RANK), BF16), v((RANK, RANK), BF16),
            v((ROWS, RANK), F32), v((ROWS, RANK), BF16), v((COLS, RANK), BF16),
            v((8, 8, RANK), F32), v((1, SHARE, RANK), BF16),
            pltpu.SemaphoreType.DMA((N_SEMS,)),
            pltpu.SemaphoreType.DMA((N_SEMS,)),
            pltpu.SemaphoreType.DMA((8,)),
        ],
        compiler_params=pltpu.CompilerParams(
            collective_id=0, has_side_effects=True, vmem_limit_bytes=60 * 2**20
        ),
        name="dion_step",
    )(momentum, gradient, right_factor, weight)


def solution(mesh):
    return jax.shard_map(
        local,
        mesh=mesh,
        in_specs=(P("fsdp", "tp"), P("fsdp", "tp"), P("tp", "fsdp", None), P("fsdp", "tp")),
        out_specs=(P("fsdp", "tp"), P("tp", "fsdp", None), P("fsdp", "tp")),
        check_vma=False,
    )
```

```python
import functools

import jax
import jax.numpy as jnp
from jax import lax
from jax.experimental import pallas as pl
from jax.experimental.pallas import tpu as pltpu
from jax.sharding import PartitionSpec as P

D = 8192
FF = 28672
RANK = 512
NX, NY, NC, NZ = 4, 8, 2, 8
ROWS = FF // (NX * NY * NC)
COLS = D // NZ
SHARE = COLS // (NX * NY * NC)
ZR = ROWS // NZ
PANELS = ((0, 0), (0, 128), (0, 256), (0, 384), (256, 256), (256, 384))
GC = 3 * 256
GX = GC // NX
GY = GX // NY
MESH = pl.DeviceIdType.MESH
HI = lax.Precision.HIGHEST
F32 = jnp.float32
BF16 = jnp.bfloat16

PHASES = {}
_n = 0
for _name, _k in (
    ("fy", 7), ("fx", 6), ("fc", 4), ("sz", 14), ("sg", 7),
    ("gc", 1), ("gx", 6), ("gy", 7), ("gz", 7), ("hy", 7), ("hx", 6), ("hc", 4),
    ("pc", 1), ("px", 6), ("py", 7), ("qy", 7), ("qx", 6), ("qc", 4), ("nz", 7),
):
    PHASES[_name] = _n
    _n += _k
N_SEMS = _n


def wide(x):
    return jnp.broadcast_to(x, (8, 128))


def diag_inverse(m, between):
    lane = lax.broadcasted_iota(jnp.int32, (8, 128), 1)
    sub = lax.broadcasted_iota(jnp.int32, (8, 128), 0)

    def pick(rows):
        row = rows[0]
        for j in range(1, 8):
            row = jnp.where(sub == j, rows[j], row)
        return row

    m = list(m)
    n = len(m)
    out = []
    for k in range(n):
        between(k)
        lo = 8 * k
        v = m[k]
        inside = (lane >= lo) & (lane < lo + 8)
        cols = [wide(v[:, lo + j : lo + j + 1]) for j in range(8)]
        a = [[wide(cols[j][i : i + 1, :]) if j <= i else None for j in range(8)] for i in range(8)]
        vi = jnp.where(inside, jnp.where(lane - lo == sub, 1.0, 0.0), v)
        vb = [wide(vi[j : j + 1, :]) for j in range(8)]
        near = range(k + 1, min(n, k + 3))
        far = k + 3
        nx = [[wide(m[b][:, lo + j : lo + j + 1]) for j in range(8)] for b in near]
        nl = [[None] * 8 for _ in near]
        new = [jnp.where(inside, 0.0, m[b]) for b in near]
        rs = [None] * 8
        r = [None] * 8
        for j in range(8):
            rs[j] = lax.rsqrt(a[j][j])
            r[j] = vb[j] * rs[j]
            for b in range(len(near)):
                nl[b][j] = nx[b][j] * rs[j]
            for i in range(j + 1, 8):
                a[i][j] = a[i][j] * rs[j]
            for i in range(j + 1, 8):
                for c in range(j + 1, i + 1):
                    a[i][c] = a[i][c] - a[i][j] * a[c][j]
                vb[i] = vb[i] - a[i][j] * r[j]
                for b in range(len(near)):
                    nx[b][i] = nx[b][i] - a[i][j] * nl[b][j]
            for b in range(len(near)):
                new[b] = new[b] - nl[b][j] * r[j]
        out.append(pick(r))
        if far < n:
            q = [None] * 8
            acc = list(r)
            for j in range(7, -1, -1):
                q[j] = acc[j] * rs[j]
                for i in range(j):
                    acc[i] = acc[i] - a[j][i] * q[j]
            padded = [jnp.zeros((8, 128), F32)] * n
            padded[k] = pick(q)
            t = jnp.dot(
                jnp.concatenate(m[far:], axis=0), jnp.concatenate(padded, axis=0),
                precision=HI, preferred_element_type=F32,
            )
            for i in range(far, n):
                m[i] = jnp.where(inside, 0.0, m[i]) - t[8 * (i - far) : 8 * (i - far) + 8, :]
        for b, i in enumerate(near):
            m[i] = new[b]
    return out


def split(x):
    hi = x.astype(BF16)
    return hi, (x - hi.astype(F32)).astype(BF16)


def dot_nt(a, b):
    return lax.dot_general(a, b, (((1,), (1,)), ((), ())), preferred_element_type=F32)


def dot_tn(a, b, precision=None):
    return lax.dot_general(
        a, b, (((0,), (0,)), ((), ())), precision=precision, preferred_element_type=F32
    )


def kernel(
    m_hbm, g_hbm, f_hbm,
    b_hbm, lh_hbm, sc_hbm, ph_hbm, fo_hbm,
    m_v, g_v, b_v, f_v, sk_v, up_v, dn_v, so_v, sa_v, sh_v, sl_v,
    gs_v, gm_v, gcr_v, gxr_v, g1_v, gyr_v, gzr_v, gg_v, ch_v,
    ps_v, pm_v, pcr_v, pxr_v, p1_v, pyr_v, pf_v,
    xh_v, xl_v, le_v, lh_v, sc_v, ph_v, nz_v, fo_v,
    send_sem, recv_sem, local_sem,
):
    i = lax.axis_index("fsdp")
    z = lax.axis_index("tp")
    c = lax.rem(i, NC)
    y = lax.rem(i // NC, NY)
    x = i // (NC * NY)

    def at(x_, y_, c_):
        return (x_ * NY + y_) * NC + c_

    def around(v, d, n):
        return lax.rem(v + d, n)

    def remote(phase, k, src, dst, fsdp, tp):
        s = PHASES[phase] + k
        return pltpu.make_async_remote_copy(
            src_ref=src, dst_ref=dst, send_sem=send_sem.at[s], recv_sem=recv_sem.at[s],
            device_id=(fsdp, tp), device_id_type=MESH,
        )

    xs = [around(x, d, NX) for d in range(NX)]
    ys = [around(y, d, NY) for d in range(NY)]
    zs = [around(z, d, NZ) for d in range(NZ)]
    other = at(x, y, 1 - c)

    def to_y(phase, src, dst):
        return [remote(phase, d - 1, src(ys[d], d), dst(ys[d], d), at(x, ys[d], c), z) for d in range(1, NY)]

    def to_z(phase, src, dst):
        return [remote(phase, d - 1, src(zs[d], d), dst(zs[d], d), i, zs[d]) for d in range(1, NZ)]

    def to_core(phase, src, dst):
        return [remote(phase, 0, src, dst, other, z)]

    def rows(ref, start, size):
        return ref.at[pl.ds(pl.multiple_of(start, 8), size)]

    def x_sums(phase, src, size, slots):
        half = size // 2

        def a(p):
            return rows(src, p * size, half)

        def b(p):
            return rows(src, p * size + half, half)

        right, left = at(xs[1], y, c), at(xs[3], y, c)
        return [
            remote(phase, 0, a(xs[2]), slots.at[0], right, z),
            remote(phase, 1, b(xs[2]), slots.at[1], left, z),
            remote(phase, 2, b(xs[1]), slots.at[2], right, z),
            remote(phase, 3, a(xs[3]), slots.at[3], left, z),
            remote(phase, 4, slots.at[0], slots.at[4], right, z),
            remote(phase, 5, slots.at[1], slots.at[5], left, z),
        ]

    def x_sums_forward(copies, src, size, slots):
        half = size // 2
        copies[0].wait_recv()
        slots[0] = slots[0] + src[pl.ds(pl.multiple_of(xs[1] * size, 8), half), :]
        copies[4].start()
        copies[1].wait_recv()
        slots[1] = slots[1] + src[pl.ds(pl.multiple_of(xs[3] * size + half, 8), half), :]
        copies[5].start()

    def x_sums_finish(copies, src, size, slots, out):
        half = size // 2
        for k in (2, 3, 4, 5):
            copies[k].wait_recv()
        out[0:half, :] = src[pl.ds(pl.multiple_of(x * size, 8), half), :] + (slots[3] + slots[4])
        out[half:size, :] = src[pl.ds(pl.multiple_of(x * size + half, 8), half), :] + (slots[2] + slots[5])

    def x_all(phase, a, b):
        right, left = at(xs[1], y, c), at(xs[3], y, c)
        return [
            remote(phase, 0, a(x), a(x), right, z),
            remote(phase, 1, b(x), b(x), left, z),
            remote(phase, 2, b(x), b(x), right, z),
            remote(phase, 3, a(x), a(x), left, z),
            remote(phase, 4, a(xs[3]), a(xs[3]), right, z),
            remote(phase, 5, b(xs[1]), b(xs[1]), left, z),
        ]

    def x_all_forward(copies):
        copies[0].wait_recv()
        copies[4].start()
        copies[1].wait_recv()
        copies[5].start()

    def x_all_finish(copies, across):
        copies[2].wait_recv()
        across[0].start()
        copies[3].wait_recv()
        across[1].start()
        copies[4].wait_recv()
        copies[5].wait_recv()
        across[2].start()

    def f_half(h):
        return lambda p: f_v.at[p, pl.ds(h * (NY // 2), NY // 2), c]

    def g_half(h):
        return lambda p: rows(gg_v, c * GC + p * GX + h * (GX // 2), GX // 2)

    def p_half(h):
        return lambda p: rows(pf_v, c * 512 + p * 128 + h * 64, 64)

    def across(phase, block):
        return [remote(phase, k, block(xs[d]), block(xs[d]), other, z) for k, d in enumerate((0, 3, 1, 2))]

    fy = to_y("fy", lambda p, d: f_v.at[x, y, c], lambda p, d: f_v.at[x, y, c])
    fx = x_all("fx", f_half(0), f_half(1))
    fc = across("fc", lambda p: f_v.at[p, :, c])

    parts = ((0, 24), (24, 32))
    up, down = [], []
    for s in range(4):
        for h, (first, size) in enumerate(parts):
            src = rows(sk_v, zs[4] * ZR + first, size) if s == 0 else up_v.at[s - 1, pl.ds(first, size)]
            up.append(remote("sz", 2 * s + h, src, up_v.at[s, pl.ds(first, size)], i, zs[1]))
    for s in range(3):
        for h, (first, size) in enumerate(parts):
            src = rows(sk_v, zs[5] * ZR + first, size) if s == 0 else dn_v.at[s - 1, pl.ds(first, size)]
            down.append(remote("sz", 8 + 2 * s + h, src, dn_v.at[s, pl.ds(first, size)], i, zs[7]))
    sg_up = []
    for s in range(4):
        piece = rows(sa_v, zs[(8 - s) % 8] * ZR, ZR)
        sg_up.append(remote("sg", s, so_v if s == 0 else piece, piece, i, zs[1]))
    sg_down = []
    for s in range(3):
        piece = rows(sa_v, zs[s] * ZR, ZR)
        sg_down.append(remote("sg", 4 + s, so_v if s == 0 else piece, piece, i, zs[7]))

    gc = to_core("gc", gs_v, gcr_v)
    gx = x_sums("gx", gm_v, GX, gxr_v)
    gy = to_y("gy", lambda p, d: rows(g1_v, p * GY, GY), lambda p, d: gyr_v.at[d - 1])
    gz = to_z("gz", lambda p, d: gzr_v.at[z], lambda p, d: gzr_v.at[z])
    g_y = rows(gg_v, c * GC + x * GX + y * GY, GY)
    hy = to_y("hy", lambda p, d: g_y, lambda p, d: g_y)
    hx = x_all("hx", g_half(0), g_half(1))
    hc = across("hc", lambda p: rows(gg_v, c * GC + p * GX, GX))
    pc = to_core("pc", ps_v, pcr_v)
    px = x_sums("px", pm_v, 128, pxr_v)
    py = to_y("py", lambda p, d: rows(p1_v, p * 16, 16), lambda p, d: pyr_v.at[d - 1])
    p_y = rows(pf_v, c * 512 + x * 128 + y * 16, 16)
    qy = to_y("qy", lambda p, d: p_y, lambda p, d: p_y)
    qx = x_all("qx", p_half(0), p_half(1))
    qc = across("qc", lambda p: rows(pf_v, c * 512 + p * 128, 128))
    nz = to_z("nz", lambda p, d: nz_v.at[z], lambda p, d: nz_v.at[z])

    def start(copies):
        for k in copies:
            k.start()

    def landed(copies):
        for k in copies:
            k.wait_recv()

    load_m = pltpu.make_async_copy(m_hbm, m_v, local_sem.at[0])
    load_g = pltpu.make_async_copy(g_hbm, g_v, local_sem.at[1])
    load_f = pltpu.make_async_copy(f_hbm.at[0], f_v.at[x, y, c], local_sem.at[2])
    load_f.start()
    load_m.start()
    load_g.start()

    barrier = pltpu.get_barrier_semaphore()
    peers = (
        [(at(xs[d], y, c), z) for d in (1, 3)]
        + [(at(x, ys[d], c), z) for d in range(1, NY)]
        + [(i, zs[d]) for d in range(1, NZ)]
        + [(other, z)]
    )
    for peer in peers:
        pl.semaphore_signal(barrier, inc=1, device_id=peer, device_id_type=MESH)
    pl.semaphore_wait(barrier, len(peers))

    load_f.wait()
    start(fy)
    load_m.wait()
    load_g.wait()

    def add_buffer(k, _):
        r = pl.ds(pl.multiple_of(k * 64, 64), 64)
        b_v[r, :] = (m_v[r, :].astype(F32) + g_v[r, :].astype(F32)).astype(BF16)
        return 0

    lax.fori_loop(0, ROWS // 64, add_buffer, 0)
    stores = [pltpu.make_async_copy(b_v, b_hbm, local_sem.at[3])]
    stores[0].start()
    landed(fy)
    start(fx[:4])
    fc[0].start()
    x_all_forward(fx)
    x_all_finish(fx, fc[1:])
    landed(fc)

    sk_v[...] = jnp.dot(b_v[...], f_v[...].reshape(COLS, RANK), preferred_element_type=F32)
    start(up[:2])
    start(down[:2])
    for s in range(1, 4):
        for h, (first, size) in enumerate(parts):
            part = pl.ds(first, size)
            up[2 * s - 2 + h].wait_recv()
            mine = pl.ds(pl.multiple_of(zs[4 - s] * ZR + first, 8), size)
            up_v[s - 1, part, :] = up_v[s - 1, part, :] + sk_v[mine, :]
            up[2 * s + h].start()
            if s < 3:
                down[2 * s - 2 + h].wait_recv()
                mine = pl.ds(pl.multiple_of(zs[5 + s] * ZR + first, 8), size)
                dn_v[s - 1, part, :] = dn_v[s - 1, part, :] + sk_v[mine, :]
                down[2 * s + h].start()
    landed(down[4:])
    landed(up[6:])
    total = sk_v[pl.ds(pl.multiple_of(z * ZR, 8), ZR), :] + (up_v[3] + dn_v[2])
    so_v[...] = total
    sg_up[0].start()
    sg_down[0].start()
    sa_v[pl.ds(pl.multiple_of(z * ZR, 8), ZR), :] = total

    def sg_forward(s):
        sg_up[s - 1].wait_recv()
        sg_up[s].start()
        if s < 3:
            sg_down[s - 1].wait_recv()
            sg_down[s].start()

    def panels(core, out):
        for j in range(3):
            n = 3 * core + j
            last = n // 4
            r = pl.ds(pl.multiple_of(256 * last, 256), 256)
            q = pl.ds(pl.multiple_of(128 * n - 256 * last, 128), 128)
            out[256 * j : 256 * j + 256, :] = dot_tn(so_v[:, r], so_v[:, q], HI)

    panels(1 - c, gs_v)
    start(gc)
    panels(c, gm_v)
    landed(gc)
    gm_v[...] = gm_v[...] + gcr_v[...]
    start(gx[:4])
    sg_forward(1)
    x_sums_forward(gx, gm_v, GX, gxr_v)
    sg_forward(2)
    x_sums_finish(gx, gm_v, GX, gxr_v, g1_v)
    start(gy)
    sg_forward(3)
    total = g1_v[pl.ds(pl.multiple_of(y * GY, 8), GY), :]
    for d in range(1, NY):
        gy[d - 1].wait_recv()
        total = total + gyr_v[d - 1]
    gzr_v[z] = total
    start(gz)

    landed(sg_up[3:])
    landed(sg_down[2:])
    sh_v[...], sl_v[...] = split(sa_v[...])

    def project(half):
        cols = pl.ds(pl.multiple_of(half * 512, 512), 512)
        return dot_tn(b_v[:, cols], sh_v[...]) + dot_tn(b_v[:, cols], sl_v[...])

    ps_v[...] = project(1 - c)
    start(pc)
    pm_v[...] = project(c)
    landed(gz)
    total = gzr_v[0]
    for d in range(1, NZ):
        total = total + gzr_v[d]
    gg_v[pl.ds(pl.multiple_of(c * GC + x * GX + y * GY, 8), GY), :] = total
    start(hy)
    landed(pc)
    pm_v[...] = pm_v[...] + pcr_v[...]
    start(px[:4])
    landed(hy)
    start(hx[:4])
    hc[0].start()
    x_sums_forward(px, pm_v, 128, pxr_v)
    x_all_forward(hx)
    x_sums_finish(px, pm_v, 128, pxr_v, p1_v)
    start(py)
    x_all_finish(hx, hc[1:])
    landed(hc)

    def progress(step):
        if step == 0:
            total = p1_v[pl.ds(pl.multiple_of(y * 16, 16), 16), :]
            for d in range(1, NY):
                py[d - 1].wait_recv()
                total = total + pyr_v[d - 1]
            pf_v[pl.ds(pl.multiple_of(c * 512 + x * 128 + y * 16, 16), 16), :] = total
            start(qy)
        elif step == 1:
            landed(qy)
            start(qx[:4])
            qc[0].start()
        elif step == 2:
            x_all_forward(qx)

    nb = RANK // 128

    ch_v[256:, :256] = jnp.zeros((256, 256), F32)
    for j, (r, q) in enumerate(PANELS):
        ch_v[r : r + 256, q : q + 128] = gg_v[256 * j : 256 * j + 256, :]
    r128 = lax.broadcasted_iota(jnp.int32, (128, 128), 0)
    c128 = lax.broadcasted_iota(jnp.int32, (128, 128), 1)

    def eliminate(k, _):
        mine = pl.ds(pl.multiple_of(k * 128, 128), 128)
        blk = ch_v[mine, mine]

        def between(j):
            for step, (outer, pivot) in enumerate(((1, 4), (2, 12), (3, 8))):
                if j == pivot:

                    @pl.when(k == outer)
                    def _():
                        progress(step)

        done = diag_inverse([blk[8 * j : 8 * j + 8, :] for j in range(16)], between)
        linv = jnp.where(r128 >= c128, jnp.concatenate(done, axis=0), 0.0)
        ch_v[mine, mine] = jnp.where(r128 == c128, 1.0, 0.0)
        ch_v[mine, :] = jnp.dot(linv, ch_v[mine, :], precision=HI, preferred_element_type=F32)
        for kk in range(nb - 1):

            @pl.when(k == kk)
            def _():
                lo, hi = 128 * kk, 128 * (kk + 1)
                ch_v[hi:, lo:hi] = jnp.zeros((RANK - hi, 128), F32)
                ch_v[hi:, :] = ch_v[hi:, :] - dot_tn(ch_v[lo:hi, hi:], ch_v[lo:hi, :], HI)

        return 0

    lax.fori_loop(0, nb, eliminate, 0)
    rr = lax.broadcasted_iota(jnp.int32, (RANK, RANK), 0)
    cc = lax.broadcasted_iota(jnp.int32, (RANK, RANK), 1)
    xh_v[...], xl_v[...] = split(jnp.where(rr >= cc, ch_v[...], 0.0))

    def times_inverse(hi, lo):
        return dot_nt(hi, xh_v[...]) + (dot_nt(hi, xl_v[...]) + dot_nt(lo, xh_v[...]))

    def store(src, dst, sem):
        stores.append(pltpu.make_async_copy(src, dst, local_sem.at[sem]))
        stores[-1].start()

    left = times_inverse(sh_v[...], sl_v[...])
    le_v[...] = left
    lh_v[...] = left.astype(BF16)
    store(lh_v, lh_hbm, 4)

    x_all_finish(qx, qc[1:])
    landed(qc)
    for copies in (qy, qx, qc):
        for k in copies:
            k.wait_send()
    proj = times_inverse(*split(pf_v[...]))
    pf_v[...] = proj
    squares = jnp.sum(jnp.sum((proj * proj).reshape(COLS // 8, 8, RANK), axis=0), axis=0, keepdims=True)
    for j in range(4):
        nz_v[z, j : j + 1, :] = squares[:, 128 * j : 128 * j + 128]
    nz_v[z, 4:8, :] = jnp.zeros((4, 128), F32)
    start(nz)
    ph_v[...] = proj.astype(BF16)
    store(ph_v, ph_hbm, 5)

    landed(nz)
    total = nz_v[0]
    for d in range(1, NZ):
        total = total + nz_v[d]
    inv = 1.0 / jnp.sqrt(total + 1e-06)
    inv = jnp.concatenate([inv[j : j + 1, :] for j in range(4)], axis=1)
    sc_v[...] = (le_v[...] * inv).astype(BF16)
    store(sc_v, sc_hbm, 6)
    fo_v[0] = (pf_v[pl.ds(pl.multiple_of(i * SHARE, SHARE), SHARE), :] * inv).astype(BF16)
    store(fo_v, fo_hbm, 7)

    for copies in (fy, fx, fc, up, down, sg_up, sg_down, gc, gx, gy, gz, hy, hx, hc, pc, px, py, nz):
        for k in copies:
            k.wait_send()
    for k in stores:
        k.wait()


def finish(b_ref, w_ref, lh_ref, sc_ref, ph_ref, f_ref, mo_ref, wo_ref, fo_ref):
    approx = dot_nt(lh_ref[...], ph_ref[...])
    mo_ref[...] = (b_ref[...].astype(F32) - 0.05 * approx).astype(BF16)
    update = dot_nt(sc_ref[...], ph_ref[...])
    scale = 0.2 * (FF * D / RANK) ** 0.5
    wo_ref[...] = (w_ref[...].astype(F32) - scale * update).astype(BF16)
    fo_ref[...] = f_ref[...]


def local(momentum, gradient, right_factor, weight):
    any_spec = pl.BlockSpec(memory_space=pl.ANY)
    v = pltpu.VMEM
    buffer, left_half, scaled_half, projected_half, factor_new = pl.pallas_call(
        kernel,
        out_shape=(
            jax.ShapeDtypeStruct((ROWS, COLS), BF16),
            jax.ShapeDtypeStruct((ROWS, RANK), BF16),
            jax.ShapeDtypeStruct((ROWS, RANK), BF16),
            jax.ShapeDtypeStruct((COLS, RANK), BF16),
            jax.ShapeDtypeStruct((1, SHARE, RANK), BF16),
        ),
        in_specs=[any_spec] * 3,
        out_specs=(any_spec,) * 5,
        scratch_shapes=[
            v((ROWS, COLS), BF16), v((ROWS, COLS), BF16), v((ROWS, COLS), BF16),
            v((NX, NY, NC, SHARE, RANK), BF16),
            v((ROWS, RANK), F32), v((4, ZR, RANK), F32), v((3, ZR, RANK), F32), v((ZR, RANK), F32), v((ROWS, RANK), F32),
            v((ROWS, RANK), BF16), v((ROWS, RANK), BF16),
            v((GC, 128), F32), v((GC, 128), F32), v((GC, 128), F32),
            v((6, GX // 2, 128), F32), v((GX, 128), F32), v((7, GY, 128), F32), v((8, GY, 128), F32),
            v((2 * GC, 128), F32), v((RANK, RANK), F32),
            v((512, RANK), F32), v((512, RANK), F32), v((512, RANK), F32),
            v((6, 64, RANK), F32), v((128, RANK), F32), v((7, 16, RANK), F32), v((COLS, RANK), F32),
            v((RANK, RANK), BF16), v((RANK, RANK), BF16),
            v((ROWS, RANK), F32), v((ROWS, RANK), BF16), v((ROWS, RANK), BF16), v((COLS, RANK), BF16),
            v((8, 8, 128), F32), v((1, SHARE, RANK), BF16),
            pltpu.SemaphoreType.DMA((N_SEMS,)),
            pltpu.SemaphoreType.DMA((N_SEMS,)),
            pltpu.SemaphoreType.DMA((8,)),
        ],
        compiler_params=pltpu.CompilerParams(
            collective_id=0, has_side_effects=True, vmem_limit_bytes=60 * 2**20
        ),
        name="dion_step",
    )(momentum, gradient, right_factor)
    tile = 256
    wide_spec = pl.BlockSpec((ROWS, tile), lambda j: (0, j))
    left_spec = pl.BlockSpec((ROWS, RANK), lambda j: (0, 0))
    share_spec = pl.BlockSpec((1, SHARE, RANK), lambda j: (0, 0, 0))
    momentum_new, weight_new, factor_new = pl.pallas_call(
        finish,
        grid=(COLS // tile,),
        out_shape=(
            jax.ShapeDtypeStruct((ROWS, COLS), BF16),
            jax.ShapeDtypeStruct((ROWS, COLS), BF16),
            jax.ShapeDtypeStruct((1, SHARE, RANK), BF16),
        ),
        in_specs=[
            wide_spec, wide_spec, left_spec, left_spec,
            pl.BlockSpec((tile, RANK), lambda j: (j, 0)), share_spec,
        ],
        out_specs=(wide_spec, wide_spec, share_spec),
        compiler_params=pltpu.CompilerParams(vmem_limit_bytes=60 * 2**20),
        name="finish",
    )(buffer, weight, left_half, scaled_half, projected_half, factor_new)
    return momentum_new, factor_new, weight_new


def solution(mesh):
    return jax.shard_map(
        local,
        mesh=mesh,
        in_specs=(P("fsdp", "tp"), P("fsdp", "tp"), P("tp", "fsdp", None), P("fsdp", "tp")),
        out_specs=(P("fsdp", "tp"), P("tp", "fsdp", None), P("fsdp", "tp")),
        check_vma=False,
    )
```

```python
import functools

import jax
import jax.numpy as jnp
from jax import lax
from jax.experimental import pallas as pl
from jax.experimental.pallas import tpu as pltpu
from jax.sharding import PartitionSpec as P

D = 8192
FF = 28672
RANK = 512
NX, NY, NC, NZ = 4, 8, 2, 8
ROWS = FF // (NX * NY * NC)
COLS = D // NZ
SHARE = COLS // (NX * NY * NC)
ZR = ROWS // NZ
HR = RANK // 2
PANELS = ((0, 0), (0, 128), (0, 256), (0, 384), (256, 256), (256, 384))
GC = 3 * 256
GX = GC // NX
GY = GX // NY
MESH = pl.DeviceIdType.MESH
HI = lax.Precision.HIGHEST
F32 = jnp.float32
BF16 = jnp.bfloat16

PHASES = {}
_n = 0
for _name, _k in (
    ("fy", 7), ("fx", 6), ("fc", 4), ("sz", 14), ("sg", 7),
    ("gc", 1), ("gx", 6), ("gy", 7), ("gz", 7), ("hy", 7), ("hx", 6), ("hc", 4),
    ("pc0", 1), ("px0", 6), ("py0", 7), ("qy0", 7), ("qx0", 6), ("qc0", 4),
    ("pc1", 1), ("px1", 6), ("py1", 7), ("qy1", 7), ("qx1", 6), ("qc1", 4), ("nz", 7),
):
    PHASES[_name] = _n
    _n += _k
N_SEMS = _n


def wide(x):
    return jnp.broadcast_to(x, (8, 128))


def diag_inverse(m, between):
    lane = lax.broadcasted_iota(jnp.int32, (8, 128), 1)
    sub = lax.broadcasted_iota(jnp.int32, (8, 128), 0)

    def pick(rows):
        row = rows[0]
        for j in range(1, 8):
            row = jnp.where(sub == j, rows[j], row)
        return row

    m = list(m)
    n = len(m)
    out = []
    for k in range(n):
        between(k)
        lo = 8 * k
        v = m[k]
        inside = (lane >= lo) & (lane < lo + 8)
        cols = [wide(v[:, lo + j : lo + j + 1]) for j in range(8)]
        a = [[wide(cols[j][i : i + 1, :]) if j <= i else None for j in range(8)] for i in range(8)]
        vi = jnp.where(inside, jnp.where(lane - lo == sub, 1.0, 0.0), v)
        vb = [wide(vi[j : j + 1, :]) for j in range(8)]
        near = range(k + 1, min(n, k + 3))
        far = k + 3
        nx = [[wide(m[b][:, lo + j : lo + j + 1]) for j in range(8)] for b in near]
        nl = [[None] * 8 for _ in near]
        new = [jnp.where(inside, 0.0, m[b]) for b in near]
        rs = [None] * 8
        r = [None] * 8
        for j in range(8):
            rs[j] = lax.rsqrt(a[j][j])
            r[j] = vb[j] * rs[j]
            for b in range(len(near)):
                nl[b][j] = nx[b][j] * rs[j]
            for i in range(j + 1, 8):
                a[i][j] = a[i][j] * rs[j]
            for i in range(j + 1, 8):
                for c in range(j + 1, i + 1):
                    a[i][c] = a[i][c] - a[i][j] * a[c][j]
                vb[i] = vb[i] - a[i][j] * r[j]
                for b in range(len(near)):
                    nx[b][i] = nx[b][i] - a[i][j] * nl[b][j]
            for b in range(len(near)):
                new[b] = new[b] - nl[b][j] * r[j]
        out.append(pick(r))
        if far < n:
            q = [None] * 8
            acc = list(r)
            for j in range(7, -1, -1):
                q[j] = acc[j] * rs[j]
                for i in range(j):
                    acc[i] = acc[i] - a[j][i] * q[j]
            padded = [jnp.zeros((8, 128), F32)] * n
            padded[k] = pick(q)
            t = jnp.dot(
                jnp.concatenate(m[far:], axis=0), jnp.concatenate(padded, axis=0),
                precision=HI, preferred_element_type=F32,
            )
            for i in range(far, n):
                m[i] = jnp.where(inside, 0.0, m[i]) - t[8 * (i - far) : 8 * (i - far) + 8, :]
        for b, i in enumerate(near):
            m[i] = new[b]
    return out


def split(x):
    hi = x.astype(BF16)
    return hi, (x - hi.astype(F32)).astype(BF16)


def dot_nt(a, b):
    return lax.dot_general(a, b, (((1,), (1,)), ((), ())), preferred_element_type=F32)


def dot_tn(a, b, precision=None):
    return lax.dot_general(
        a, b, (((0,), (0,)), ((), ())), precision=precision, preferred_element_type=F32
    )


def kernel(
    m_hbm, g_hbm, f_hbm,
    b_hbm, lh_hbm, sc_hbm, ph_hbm, fo_hbm,
    m_v, g_v, b_v, f_v, sk_v, up_v, dn_v, so_v, sa_v, sh_v, sl_v,
    gs_v, gm_v, gcr_v, gxr_v, g1_v, gyr_v, gzr_v, gg_v, ch_v,
    ps_v, pm_v, pcr_v, pxr_v, p1_v, pyr_v, pf_v, pr_v,
    xh_v, xl_v, le_v, lh_v, sc_v, ph_v, nz_v, fo_v,
    send_sem, recv_sem, local_sem,
):
    i = lax.axis_index("fsdp")
    z = lax.axis_index("tp")
    c = lax.rem(i, NC)
    y = lax.rem(i // NC, NY)
    x = i // (NC * NY)

    def at(x_, y_, c_):
        return (x_ * NY + y_) * NC + c_

    def around(v, d, n):
        return lax.rem(v + d, n)

    def remote(phase, k, src, dst, fsdp, tp):
        s = PHASES[phase] + k
        return pltpu.make_async_remote_copy(
            src_ref=src, dst_ref=dst, send_sem=send_sem.at[s], recv_sem=recv_sem.at[s],
            device_id=(fsdp, tp), device_id_type=MESH,
        )

    xs = [around(x, d, NX) for d in range(NX)]
    ys = [around(y, d, NY) for d in range(NY)]
    zs = [around(z, d, NZ) for d in range(NZ)]
    other = at(x, y, 1 - c)

    def to_y(phase, src, dst):
        return [remote(phase, d - 1, src(ys[d], d), dst(ys[d], d), at(x, ys[d], c), z) for d in range(1, NY)]

    def to_z(phase, src, dst):
        return [remote(phase, d - 1, src(zs[d], d), dst(zs[d], d), i, zs[d]) for d in range(1, NZ)]

    def to_core(phase, src, dst):
        return [remote(phase, 0, src, dst, other, z)]

    def rows(ref, start, size):
        return ref.at[pl.ds(pl.multiple_of(start, 8), size)]

    def x_sums(phase, src, size, slots):
        half = size // 2

        def a(p):
            return rows(src, p * size, half)

        def b(p):
            return rows(src, p * size + half, half)

        right, left = at(xs[1], y, c), at(xs[3], y, c)
        return [
            remote(phase, 0, a(xs[2]), slots.at[0], right, z),
            remote(phase, 1, b(xs[2]), slots.at[1], left, z),
            remote(phase, 2, b(xs[1]), slots.at[2], right, z),
            remote(phase, 3, a(xs[3]), slots.at[3], left, z),
            remote(phase, 4, slots.at[0], slots.at[4], right, z),
            remote(phase, 5, slots.at[1], slots.at[5], left, z),
        ]

    def x_sums_forward(copies, src, size, slots):
        half = size // 2
        copies[0].wait_recv()
        slots[0] = slots[0] + src[pl.ds(pl.multiple_of(xs[1] * size, 8), half), :]
        copies[4].start()
        copies[1].wait_recv()
        slots[1] = slots[1] + src[pl.ds(pl.multiple_of(xs[3] * size + half, 8), half), :]
        copies[5].start()

    def x_sums_finish(copies, src, size, slots, out):
        half = size // 2
        for k in (2, 3, 4, 5):
            copies[k].wait_recv()
        out[0:half, :] = src[pl.ds(pl.multiple_of(x * size, 8), half), :] + (slots[3] + slots[4])
        out[half:size, :] = src[pl.ds(pl.multiple_of(x * size + half, 8), half), :] + (slots[2] + slots[5])

    def x_all(phase, a, b):
        right, left = at(xs[1], y, c), at(xs[3], y, c)
        return [
            remote(phase, 0, a(x), a(x), right, z),
            remote(phase, 1, b(x), b(x), left, z),
            remote(phase, 2, b(x), b(x), right, z),
            remote(phase, 3, a(x), a(x), left, z),
            remote(phase, 4, a(xs[3]), a(xs[3]), right, z),
            remote(phase, 5, b(xs[1]), b(xs[1]), left, z),
        ]

    def x_all_forward(copies):
        copies[0].wait_recv()
        copies[4].start()
        copies[1].wait_recv()
        copies[5].start()

    def x_all_finish(copies, across):
        copies[2].wait_recv()
        across[0].start()
        copies[3].wait_recv()
        across[1].start()
        copies[4].wait_recv()
        copies[5].wait_recv()
        across[2].start()

    def f_half(h):
        return lambda p: f_v.at[p, pl.ds(h * (NY // 2), NY // 2), c]

    def g_half(h):
        return lambda p: rows(gg_v, c * GC + p * GX + h * (GX // 2), GX // 2)

    def across(phase, block):
        return [remote(phase, k, block(xs[d]), block(xs[d]), other, z) for k, d in enumerate((0, 3, 1, 2))]

    fy = to_y("fy", lambda p, d: f_v.at[x, y, c], lambda p, d: f_v.at[x, y, c])
    fx = x_all("fx", f_half(0), f_half(1))
    fc = across("fc", lambda p: f_v.at[p, :, c])

    parts = ((0, 24), (24, 32))
    up, down = [], []
    for s in range(4):
        for h, (first, size) in enumerate(parts):
            src = rows(sk_v, zs[4] * ZR + first, size) if s == 0 else up_v.at[s - 1, pl.ds(first, size)]
            up.append(remote("sz", 2 * s + h, src, up_v.at[s, pl.ds(first, size)], i, zs[1]))
    for s in range(3):
        for h, (first, size) in enumerate(parts):
            src = rows(sk_v, zs[5] * ZR + first, size) if s == 0 else dn_v.at[s - 1, pl.ds(first, size)]
            down.append(remote("sz", 8 + 2 * s + h, src, dn_v.at[s, pl.ds(first, size)], i, zs[7]))
    sg_up = []
    for s in range(4):
        piece = rows(sa_v, zs[(8 - s) % 8] * ZR, ZR)
        sg_up.append(remote("sg", s, so_v if s == 0 else piece, piece, i, zs[1]))
    sg_down = []
    for s in range(3):
        piece = rows(sa_v, zs[s] * ZR, ZR)
        sg_down.append(remote("sg", 4 + s, so_v if s == 0 else piece, piece, i, zs[7]))

    gc = to_core("gc", gs_v, gcr_v)
    gx = x_sums("gx", gm_v, GX, gxr_v)
    gy = to_y("gy", lambda p, d: rows(g1_v, p * GY, GY), lambda p, d: gyr_v.at[d - 1])
    gz = to_z("gz", lambda p, d: gzr_v.at[z], lambda p, d: gzr_v.at[z])
    g_y = rows(gg_v, c * GC + x * GX + y * GY, GY)
    hy = to_y("hy", lambda p, d: g_y, lambda p, d: g_y)
    hx = x_all("hx", g_half(0), g_half(1))
    hc = across("hc", lambda p: rows(gg_v, c * GC + p * GX, GX))
    def projection_copies(j):
        p_y = rows(pf_v.at[j], c * 512 + x * 128 + y * 16, 16)

        def half(h):
            return lambda p: rows(pf_v.at[j], c * 512 + p * 128 + h * 64, 64)

        return (
            to_core(f"pc{j}", ps_v.at[j], pcr_v.at[j]),
            x_sums(f"px{j}", pm_v.at[j], 128, pxr_v.at[j]),
            to_y(f"py{j}", lambda p, d: rows(p1_v.at[j], p * 16, 16), lambda p, d: pyr_v.at[j, d - 1]),
            to_y(f"qy{j}", lambda p, d: p_y, lambda p, d: p_y),
            x_all(f"qx{j}", half(0), half(1)),
            across(f"qc{j}", lambda p: rows(pf_v.at[j], c * 512 + p * 128, 128)),
        )

    pc, px, py, qy, qx, qc = zip(projection_copies(0), projection_copies(1))
    nz = to_z("nz", lambda p, d: nz_v.at[z], lambda p, d: nz_v.at[z])

    def start(copies):
        for k in copies:
            k.start()

    def landed(copies):
        for k in copies:
            k.wait_recv()

    load_m = pltpu.make_async_copy(m_hbm, m_v, local_sem.at[0])
    load_g = pltpu.make_async_copy(g_hbm, g_v, local_sem.at[1])
    load_f = pltpu.make_async_copy(f_hbm.at[0], f_v.at[x, y, c], local_sem.at[2])
    load_f.start()
    load_m.start()
    load_g.start()

    barrier = pltpu.get_barrier_semaphore()
    peers = (
        [(at(xs[d], y, c), z) for d in (1, 3)]
        + [(at(x, ys[d], c), z) for d in range(1, NY)]
        + [(i, zs[d]) for d in range(1, NZ)]
        + [(other, z)]
    )
    for peer in peers:
        pl.semaphore_signal(barrier, inc=1, device_id=peer, device_id_type=MESH)
    pl.semaphore_wait(barrier, len(peers))

    load_f.wait()
    start(fy)
    load_m.wait()
    load_g.wait()

    def add_buffer(k, _):
        r = pl.ds(pl.multiple_of(k * 64, 64), 64)
        b_v[r, :] = (m_v[r, :].astype(F32) + g_v[r, :].astype(F32)).astype(BF16)
        return 0

    lax.fori_loop(0, ROWS // 64, add_buffer, 0)
    stores = [pltpu.make_async_copy(b_v, b_hbm, local_sem.at[3])]
    stores[0].start()
    landed(fy)
    start(fx[:4])
    fc[0].start()
    x_all_forward(fx)
    x_all_finish(fx, fc[1:])
    landed(fc)

    sk_v[...] = jnp.dot(b_v[...], f_v[...].reshape(COLS, RANK), preferred_element_type=F32)
    start(up[:2])
    start(down[:2])
    for s in range(1, 4):
        for h, (first, size) in enumerate(parts):
            part = pl.ds(first, size)
            up[2 * s - 2 + h].wait_recv()
            mine = pl.ds(pl.multiple_of(zs[4 - s] * ZR + first, 8), size)
            up_v[s - 1, part, :] = up_v[s - 1, part, :] + sk_v[mine, :]
            up[2 * s + h].start()
            if s < 3:
                down[2 * s - 2 + h].wait_recv()
                mine = pl.ds(pl.multiple_of(zs[5 + s] * ZR + first, 8), size)
                dn_v[s - 1, part, :] = dn_v[s - 1, part, :] + sk_v[mine, :]
                down[2 * s + h].start()
    landed(down[4:])
    landed(up[6:])
    total = sk_v[pl.ds(pl.multiple_of(z * ZR, 8), ZR), :] + (up_v[3] + dn_v[2])
    so_v[...] = total
    sg_up[0].start()
    sg_down[0].start()
    sa_v[pl.ds(pl.multiple_of(z * ZR, 8), ZR), :] = total

    def sg_forward(s):
        sg_up[s - 1].wait_recv()
        sg_up[s].start()
        if s < 3:
            sg_down[s - 1].wait_recv()
            sg_down[s].start()

    def panels(core, out):
        for j in range(3):
            n = 3 * core + j
            last = n // 4
            r = pl.ds(pl.multiple_of(256 * last, 256), 256)
            q = pl.ds(pl.multiple_of(128 * n - 256 * last, 128), 128)
            out[256 * j : 256 * j + 256, :] = dot_tn(so_v[:, r], so_v[:, q], HI)

    panels(1 - c, gs_v)
    start(gc)
    panels(c, gm_v)
    landed(gc)
    gm_v[...] = gm_v[...] + gcr_v[...]
    start(gx[:4])
    sg_forward(1)
    x_sums_forward(gx, gm_v, GX, gxr_v)
    sg_forward(2)
    x_sums_finish(gx, gm_v, GX, gxr_v, g1_v)
    start(gy)
    sg_forward(3)
    total = g1_v[pl.ds(pl.multiple_of(y * GY, 8), GY), :]
    for d in range(1, NY):
        gy[d - 1].wait_recv()
        total = total + gyr_v[d - 1]
    gzr_v[z] = total
    start(gz)

    landed(sg_up[3:])
    landed(sg_down[2:])
    sh_v[...], sl_v[...] = split(sa_v[...])

    def project(half, j):
        cols = pl.ds(pl.multiple_of(half * 512, 512), 512)
        part = slice(HR * j, HR * j + HR)
        return dot_tn(b_v[:, cols], sh_v[:, part]) + dot_tn(b_v[:, cols], sl_v[:, part])

    for j in range(2):
        ps_v[j] = project(1 - c, j)
        start(pc[j])
    for j in range(2):
        pm_v[j] = project(c, j)
    landed(gz)
    total = gzr_v[0]
    for d in range(1, NZ):
        total = total + gzr_v[d]
    gg_v[pl.ds(pl.multiple_of(c * GC + x * GX + y * GY, 8), GY), :] = total
    start(hy)

    def px_start(j):
        landed(pc[j])
        pm_v[j] = pm_v[j] + pcr_v[j]
        start(px[j][:4])

    def px_forward(j):
        x_sums_forward(px[j], pm_v.at[j], 128, pxr_v.at[j])

    def px_finish(j):
        x_sums_finish(px[j], pm_v.at[j], 128, pxr_v.at[j], p1_v.at[j])
        start(py[j])

    def py_finish(j):
        total = p1_v[j, pl.ds(pl.multiple_of(y * 16, 16), 16), :]
        for d in range(1, NY):
            py[j][d - 1].wait_recv()
            total = total + pyr_v[j, d - 1]
        pf_v[j, pl.ds(pl.multiple_of(c * 512 + x * 128 + y * 16, 16), 16), :] = total
        start(qy[j])

    def qy_finish(j):
        landed(qy[j])
        start(qx[j][:4])
        qc[j][0].start()

    px_start(0)
    px_start(1)
    px_forward(0)
    landed(hy)
    start(hx[:4])
    hc[0].start()
    px_forward(1)
    x_all_forward(hx)
    px_finish(0)
    x_all_finish(hx, hc[1:])
    px_finish(1)
    landed(hc)

    steps = (
        (0, 3, lambda: py_finish(0)),
        (1, 0, lambda: py_finish(1)),
        (1, 9, lambda: qy_finish(0)),
        (2, 6, lambda: x_all_forward(qx[0])),
        (2, 7, lambda: qy_finish(1)),
        (2, 14, lambda: x_all_finish(qx[0], qc[0][1:])),
        (3, 6, lambda: x_all_forward(qx[1])),
        (3, 14, lambda: x_all_finish(qx[1], qc[1][1:])),
    )

    nb = RANK // 128

    ch_v[256:, :256] = jnp.zeros((256, 256), F32)
    for j, (r, q) in enumerate(PANELS):
        ch_v[r : r + 256, q : q + 128] = gg_v[256 * j : 256 * j + 256, :]
    r128 = lax.broadcasted_iota(jnp.int32, (128, 128), 0)
    c128 = lax.broadcasted_iota(jnp.int32, (128, 128), 1)

    def eliminate(k, _):
        mine = pl.ds(pl.multiple_of(k * 128, 128), 128)
        blk = ch_v[mine, mine]

        def between(j):
            for outer, pivot, step in steps:
                if j == pivot:
                    pl.when(k == outer)(step)

        done = diag_inverse([blk[8 * j : 8 * j + 8, :] for j in range(16)], between)
        linv = jnp.where(r128 >= c128, jnp.concatenate(done, axis=0), 0.0)
        ch_v[mine, mine] = jnp.where(r128 == c128, 1.0, 0.0)
        ch_v[mine, :] = jnp.dot(linv, ch_v[mine, :], precision=HI, preferred_element_type=F32)
        for kk in range(nb - 1):

            @pl.when(k == kk)
            def _():
                lo, hi = 128 * kk, 128 * (kk + 1)
                ch_v[hi:, lo:hi] = jnp.zeros((RANK - hi, 128), F32)
                ch_v[hi:, :] = ch_v[hi:, :] - dot_tn(ch_v[lo:hi, hi:], ch_v[lo:hi, :], HI)

        return 0

    lax.fori_loop(0, nb, eliminate, 0)
    rr = lax.broadcasted_iota(jnp.int32, (RANK, RANK), 0)
    cc = lax.broadcasted_iota(jnp.int32, (RANK, RANK), 1)
    xh_v[...], xl_v[...] = split(jnp.where(rr >= cc, ch_v[...], 0.0))

    def times_inverse(hi, lo):
        return dot_nt(hi, xh_v[...]) + (dot_nt(hi, xl_v[...]) + dot_nt(lo, xh_v[...]))

    def store(src, dst, sem):
        stores.append(pltpu.make_async_copy(src, dst, local_sem.at[sem]))
        stores[-1].start()

    def projected(half):
        r = pl.ds(pl.multiple_of(half * 512, 512), 512)
        proj = times_inverse(*split(jnp.concatenate([pf_v[0, r, :], pf_v[1, r, :]], axis=1)))
        pr_v[r, :] = proj
        ph_v[r, :] = proj.astype(BF16)
        return jnp.sum((proj * proj).reshape(64, 8, RANK), axis=0)

    squares = projected(c)
    landed(qc[0])
    landed(qc[1])
    squares = jnp.sum(squares + projected(1 - c), axis=0, keepdims=True)
    for j in range(4):
        nz_v[z, j : j + 1, :] = squares[:, 128 * j : 128 * j + 128]
    nz_v[z, 4:8, :] = jnp.zeros((4, 128), F32)
    start(nz)
    store(ph_v, ph_hbm, 5)
    left = times_inverse(sh_v[...], sl_v[...])
    le_v[...] = left
    lh_v[...] = left.astype(BF16)
    store(lh_v, lh_hbm, 4)

    landed(nz)
    total = nz_v[0]
    for d in range(1, NZ):
        total = total + nz_v[d]
    inv = 1.0 / jnp.sqrt(total + 1e-06)
    inv = jnp.concatenate([inv[j : j + 1, :] for j in range(4)], axis=1)
    sc_v[...] = (le_v[...] * inv).astype(BF16)
    store(sc_v, sc_hbm, 6)
    fo_v[0] = (pr_v[pl.ds(pl.multiple_of(i * SHARE, SHARE), SHARE), :] * inv).astype(BF16)
    store(fo_v, fo_hbm, 7)

    for copies in (fy, fx, fc, up, down, sg_up, sg_down, gc, gx, gy, gz, hy, hx, hc, *pc, *px, *py, *qy, *qx, *qc, nz):
        for k in copies:
            k.wait_send()
    for k in stores:
        k.wait()


def finish(b_ref, w_ref, lh_ref, sc_ref, ph_ref, f_ref, mo_ref, wo_ref, fo_ref):
    approx = dot_nt(lh_ref[...], ph_ref[...])
    mo_ref[...] = (b_ref[...].astype(F32) - 0.05 * approx).astype(BF16)
    update = dot_nt(sc_ref[...], ph_ref[...])
    scale = 0.2 * (FF * D / RANK) ** 0.5
    wo_ref[...] = (w_ref[...].astype(F32) - scale * update).astype(BF16)
    fo_ref[...] = f_ref[...]


def local(momentum, gradient, right_factor, weight):
    any_spec = pl.BlockSpec(memory_space=pl.ANY)
    v = pltpu.VMEM
    buffer, left_half, scaled_half, projected_half, factor_new = pl.pallas_call(
        kernel,
        out_shape=(
            jax.ShapeDtypeStruct((ROWS, COLS), BF16),
            jax.ShapeDtypeStruct((ROWS, RANK), BF16),
            jax.ShapeDtypeStruct((ROWS, RANK), BF16),
            jax.ShapeDtypeStruct((COLS, RANK), BF16),
            jax.ShapeDtypeStruct((1, SHARE, RANK), BF16),
        ),
        in_specs=[any_spec] * 3,
        out_specs=(any_spec,) * 5,
        scratch_shapes=[
            v((ROWS, COLS), BF16), v((ROWS, COLS), BF16), v((ROWS, COLS), BF16),
            v((NX, NY, NC, SHARE, RANK), BF16),
            v((ROWS, RANK), F32), v((4, ZR, RANK), F32), v((3, ZR, RANK), F32), v((ZR, RANK), F32), v((ROWS, RANK), F32),
            v((ROWS, RANK), BF16), v((ROWS, RANK), BF16),
            v((GC, 128), F32), v((GC, 128), F32), v((GC, 128), F32),
            v((6, GX // 2, 128), F32), v((GX, 128), F32), v((7, GY, 128), F32), v((8, GY, 128), F32),
            v((2 * GC, 128), F32), v((RANK, RANK), F32),
            v((2, 512, HR), F32), v((2, 512, HR), F32), v((2, 512, HR), F32),
            v((2, 6, 64, HR), F32), v((2, 128, HR), F32), v((2, 7, 16, HR), F32), v((2, COLS, HR), F32),
            v((COLS, RANK), F32),
            v((RANK, RANK), BF16), v((RANK, RANK), BF16),
            v((ROWS, RANK), F32), v((ROWS, RANK), BF16), v((ROWS, RANK), BF16), v((COLS, RANK), BF16),
            v((8, 8, 128), F32), v((1, SHARE, RANK), BF16),
            pltpu.SemaphoreType.DMA((N_SEMS,)),
            pltpu.SemaphoreType.DMA((N_SEMS,)),
            pltpu.SemaphoreType.DMA((8,)),
        ],
        compiler_params=pltpu.CompilerParams(
            collective_id=0, has_side_effects=True, vmem_limit_bytes=60 * 2**20
        ),
        name="dion_step",
    )(momentum, gradient, right_factor)
    tile = 512
    wide_spec = pl.BlockSpec((ROWS, tile), lambda j: (0, j))
    left_spec = pl.BlockSpec((ROWS, RANK), lambda j: (0, 0))
    share_spec = pl.BlockSpec((1, SHARE, RANK), lambda j: (0, 0, 0))
    momentum_new, weight_new, factor_new = pl.pallas_call(
        finish,
        grid=(COLS // tile,),
        out_shape=(
            jax.ShapeDtypeStruct((ROWS, COLS), BF16),
            jax.ShapeDtypeStruct((ROWS, COLS), BF16),
            jax.ShapeDtypeStruct((1, SHARE, RANK), BF16),
        ),
        in_specs=[
            wide_spec, wide_spec, left_spec, left_spec,
            pl.BlockSpec((tile, RANK), lambda j: (j, 0)), share_spec,
        ],
        out_specs=(wide_spec, wide_spec, share_spec),
        compiler_params=pltpu.CompilerParams(vmem_limit_bytes=60 * 2**20),
        name="finish",
    )(buffer, weight, left_half, scaled_half, projected_half, factor_new)
    return momentum_new, factor_new, weight_new


def solution(mesh):
    return jax.shard_map(
        local,
        mesh=mesh,
        in_specs=(P("fsdp", "tp"), P("fsdp", "tp"), P("tp", "fsdp", None), P("fsdp", "tp")),
        out_specs=(P("fsdp", "tp"), P("tp", "fsdp", None), P("fsdp", "tp")),
        check_vma=False,
    )
```

```python
import functools

import jax
import jax.numpy as jnp
from jax import lax
from jax.experimental import pallas as pl
from jax.experimental.pallas import tpu as pltpu
from jax.sharding import PartitionSpec as P

D = 8192
FF = 28672
RANK = 512
NX, NY, NC, NZ = 4, 8, 2, 8
ROWS = FF // (NX * NY * NC)
COLS = D // NZ
SHARE = COLS // (NX * NY * NC)
ZR = ROWS // NZ
HR = RANK // 2
PANELS = ((0, 0), (0, 128), (0, 256), (0, 384), (256, 256), (256, 384))
GC = 3 * 256
GX = GC // NX
GY = GX // NY
MESH = pl.DeviceIdType.MESH
HI = lax.Precision.HIGHEST
F32 = jnp.float32
BF16 = jnp.bfloat16

PHASES = {}
_n = 0
for _name, _k in (
    ("fy", 7), ("fx", 6), ("fc", 4), ("sz", 14), ("sg", 7),
    ("gc", 1), ("gx", 6), ("gy", 7), ("gz", 7), ("hy", 7), ("hx", 6), ("hc", 4),
    ("pc0", 1), ("px0", 6), ("py0", 7), ("qy0", 7), ("qx0", 6), ("qc0", 4),
    ("pc1", 1), ("px1", 6), ("py1", 7), ("qy1", 7), ("qx1", 6), ("qc1", 4), ("nz", 7),
):
    PHASES[_name] = _n
    _n += _k
N_SEMS = _n


def wide(x):
    return jnp.broadcast_to(x, (8, 128))


def diag_inverse(m, between):
    lane = lax.broadcasted_iota(jnp.int32, (8, 128), 1)
    sub = lax.broadcasted_iota(jnp.int32, (8, 128), 0)

    def pick(rows):
        row = rows[0]
        for j in range(1, 8):
            row = jnp.where(sub == j, rows[j], row)
        return row

    m = list(m)
    n = len(m)
    out = []
    for k in range(n):
        between(k)
        lo = 8 * k
        v = m[k]
        inside = (lane >= lo) & (lane < lo + 8)
        cols = [wide(v[:, lo + j : lo + j + 1]) for j in range(8)]
        a = [[wide(cols[j][i : i + 1, :]) if j <= i else None for j in range(8)] for i in range(8)]
        vi = jnp.where(inside, jnp.where(lane - lo == sub, 1.0, 0.0), v)
        vb = [wide(vi[j : j + 1, :]) for j in range(8)]
        near = range(k + 1, min(n, k + 3))
        far = k + 3
        nx = [[wide(m[b][:, lo + j : lo + j + 1]) for j in range(8)] for b in near]
        nl = [[None] * 8 for _ in near]
        new = [jnp.where(inside, 0.0, m[b]) for b in near]
        rs = [None] * 8
        r = [None] * 8
        for j in range(8):
            rs[j] = lax.rsqrt(a[j][j])
            r[j] = vb[j] * rs[j]
            for b in range(len(near)):
                nl[b][j] = nx[b][j] * rs[j]
            for i in range(j + 1, 8):
                a[i][j] = a[i][j] * rs[j]
            for i in range(j + 1, 8):
                for c in range(j + 1, i + 1):
                    a[i][c] = a[i][c] - a[i][j] * a[c][j]
                vb[i] = vb[i] - a[i][j] * r[j]
                for b in range(len(near)):
                    nx[b][i] = nx[b][i] - a[i][j] * nl[b][j]
            for b in range(len(near)):
                new[b] = new[b] - nl[b][j] * r[j]
        out.append(pick(r))
        if far < n:
            q = [None] * 8
            acc = list(r)
            for j in range(7, -1, -1):
                q[j] = acc[j] * rs[j]
                for i in range(j):
                    acc[i] = acc[i] - a[j][i] * q[j]
            padded = [jnp.zeros((8, 128), F32)] * n
            padded[k] = pick(q)
            t = jnp.dot(
                jnp.concatenate(m[far:], axis=0), jnp.concatenate(padded, axis=0),
                precision=HI, preferred_element_type=F32,
            )
            for i in range(far, n):
                m[i] = jnp.where(inside, 0.0, m[i]) - t[8 * (i - far) : 8 * (i - far) + 8, :]
        for b, i in enumerate(near):
            m[i] = new[b]
    return out


def split(x):
    hi = x.astype(BF16)
    return hi, (x - hi.astype(F32)).astype(BF16)


def dot_nt(a, b):
    return lax.dot_general(a, b, (((1,), (1,)), ((), ())), preferred_element_type=F32)


def dot_tn(a, b, precision=None):
    return lax.dot_general(
        a, b, (((0,), (0,)), ((), ())), precision=precision, preferred_element_type=F32
    )


def kernel(
    m_hbm, g_hbm, f_hbm,
    b_hbm, lh_hbm, sc_hbm, ph_hbm, fo_hbm,
    m_v, g_v, b_v, f_v, sk_v, up_v, dn_v, so_v, sa_v, sh_v, sl_v,
    gs_v, gm_v, gcr_v, gxr_v, g1_v, gyr_v, gzr_v, gg_v, ch_v,
    ps_v, pm_v, pcr_v, pxr_v, p1_v, pyr_v, pf_v, pr_v,
    xh_v, xl_v, le_v, lh_v, sc_v, ph_v, nz_v, fo_v,
    send_sem, recv_sem, local_sem,
):
    i = lax.axis_index("fsdp")
    z = lax.axis_index("tp")
    c = lax.rem(i, NC)
    y = lax.rem(i // NC, NY)
    x = i // (NC * NY)

    def at(x_, y_, c_):
        return (x_ * NY + y_) * NC + c_

    def around(v, d, n):
        return lax.rem(v + d, n)

    def remote(phase, k, src, dst, fsdp, tp):
        s = PHASES[phase] + k
        return pltpu.make_async_remote_copy(
            src_ref=src, dst_ref=dst, send_sem=send_sem.at[s], recv_sem=recv_sem.at[s],
            device_id=(fsdp, tp), device_id_type=MESH,
        )

    xs = [around(x, d, NX) for d in range(NX)]
    ys = [around(y, d, NY) for d in range(NY)]
    zs = [around(z, d, NZ) for d in range(NZ)]
    other = at(x, y, 1 - c)

    def to_y(phase, src, dst):
        return [remote(phase, d - 1, src(ys[d], d), dst(ys[d], d), at(x, ys[d], c), z) for d in range(1, NY)]

    def to_z(phase, src, dst):
        return [remote(phase, d - 1, src(zs[d], d), dst(zs[d], d), i, zs[d]) for d in range(1, NZ)]

    def to_core(phase, src, dst):
        return [remote(phase, 0, src, dst, other, z)]

    def rows(ref, start, size):
        return ref.at[pl.ds(pl.multiple_of(start, 8), size)]

    def x_sums(phase, src, size, slots):
        half = size // 2

        def a(p):
            return rows(src, p * size, half)

        def b(p):
            return rows(src, p * size + half, half)

        right, left = at(xs[1], y, c), at(xs[3], y, c)
        return [
            remote(phase, 0, a(xs[2]), slots.at[0], right, z),
            remote(phase, 1, b(xs[2]), slots.at[1], left, z),
            remote(phase, 2, b(xs[1]), slots.at[2], right, z),
            remote(phase, 3, a(xs[3]), slots.at[3], left, z),
            remote(phase, 4, slots.at[0], slots.at[4], right, z),
            remote(phase, 5, slots.at[1], slots.at[5], left, z),
        ]

    def x_sums_forward(copies, src, size, slots):
        half = size // 2
        copies[0].wait_recv()
        slots[0] = slots[0] + src[pl.ds(pl.multiple_of(xs[1] * size, 8), half), :]
        copies[4].start()
        copies[1].wait_recv()
        slots[1] = slots[1] + src[pl.ds(pl.multiple_of(xs[3] * size + half, 8), half), :]
        copies[5].start()

    def x_sums_finish(copies, src, size, slots, out):
        half = size // 2
        for k in (2, 3, 4, 5):
            copies[k].wait_recv()
        out[0:half, :] = src[pl.ds(pl.multiple_of(x * size, 8), half), :] + (slots[3] + slots[4])
        out[half:size, :] = src[pl.ds(pl.multiple_of(x * size + half, 8), half), :] + (slots[2] + slots[5])

    def x_all(phase, a, b):
        right, left = at(xs[1], y, c), at(xs[3], y, c)
        return [
            remote(phase, 0, a(x), a(x), right, z),
            remote(phase, 1, b(x), b(x), left, z),
            remote(phase, 2, b(x), b(x), right, z),
            remote(phase, 3, a(x), a(x), left, z),
            remote(phase, 4, a(xs[3]), a(xs[3]), right, z),
            remote(phase, 5, b(xs[1]), b(xs[1]), left, z),
        ]

    def x_all_forward(copies):
        copies[0].wait_recv()
        copies[4].start()
        copies[1].wait_recv()
        copies[5].start()

    def x_all_finish(copies, across):
        copies[2].wait_recv()
        across[0].start()
        copies[3].wait_recv()
        across[1].start()
        copies[4].wait_recv()
        copies[5].wait_recv()
        across[2].start()

    def f_half(h):
        return lambda p: f_v.at[p, pl.ds(h * (NY // 2), NY // 2), c]

    def g_half(h):
        return lambda p: rows(gg_v, c * GC + p * GX + h * (GX // 2), GX // 2)

    def across(phase, block):
        return [remote(phase, k, block(xs[d]), block(xs[d]), other, z) for k, d in enumerate((0, 3, 1, 2))]

    fy = to_y("fy", lambda p, d: f_v.at[x, y, c], lambda p, d: f_v.at[x, y, c])
    fx = x_all("fx", f_half(0), f_half(1))
    fc = across("fc", lambda p: f_v.at[p, :, c])

    parts = ((0, 24), (24, 32))
    up, down = [], []
    for s in range(4):
        for h, (first, size) in enumerate(parts):
            src = rows(sk_v, zs[4] * ZR + first, size) if s == 0 else up_v.at[s - 1, pl.ds(first, size)]
            up.append(remote("sz", 2 * s + h, src, up_v.at[s, pl.ds(first, size)], i, zs[1]))
    for s in range(3):
        for h, (first, size) in enumerate(parts):
            src = rows(sk_v, zs[5] * ZR + first, size) if s == 0 else dn_v.at[s - 1, pl.ds(first, size)]
            down.append(remote("sz", 8 + 2 * s + h, src, dn_v.at[s, pl.ds(first, size)], i, zs[7]))
    sg_up = []
    for s in range(4):
        piece = rows(sa_v, zs[(8 - s) % 8] * ZR, ZR)
        sg_up.append(remote("sg", s, so_v if s == 0 else piece, piece, i, zs[1]))
    sg_down = []
    for s in range(3):
        piece = rows(sa_v, zs[s] * ZR, ZR)
        sg_down.append(remote("sg", 4 + s, so_v if s == 0 else piece, piece, i, zs[7]))

    gc = to_core("gc", gs_v, gcr_v)
    gx = x_sums("gx", gm_v, GX, gxr_v)
    gy = to_y("gy", lambda p, d: rows(g1_v, p * GY, GY), lambda p, d: gyr_v.at[d - 1])
    gz = to_z("gz", lambda p, d: gzr_v.at[z], lambda p, d: gzr_v.at[z])
    g_y = rows(gg_v, c * GC + x * GX + y * GY, GY)
    hy = to_y("hy", lambda p, d: g_y, lambda p, d: g_y)
    hx = x_all("hx", g_half(0), g_half(1))
    hc = across("hc", lambda p: rows(gg_v, c * GC + p * GX, GX))
    def projection_copies(j):
        p_y = rows(pf_v.at[j], c * 512 + x * 128 + y * 16, 16)

        def half(h):
            return lambda p: rows(pf_v.at[j], c * 512 + p * 128 + h * 64, 64)

        return (
            to_core(f"pc{j}", ps_v.at[j], pcr_v.at[j]),
            x_sums(f"px{j}", pm_v.at[j], 128, pxr_v.at[j]),
            to_y(f"py{j}", lambda p, d: rows(p1_v.at[j], p * 16, 16), lambda p, d: pyr_v.at[j, d - 1]),
            to_y(f"qy{j}", lambda p, d: p_y, lambda p, d: p_y),
            x_all(f"qx{j}", half(0), half(1)),
            across(f"qc{j}", lambda p: rows(pf_v.at[j], c * 512 + p * 128, 128)),
        )

    pc, px, py, qy, qx, qc = zip(projection_copies(0), projection_copies(1))
    nz = to_z("nz", lambda p, d: nz_v.at[z], lambda p, d: nz_v.at[z])

    def start(copies):
        for k in copies:
            k.start()

    def landed(copies):
        for k in copies:
            k.wait_recv()

    load_m = pltpu.make_async_copy(m_hbm, m_v, local_sem.at[0])
    load_g = pltpu.make_async_copy(g_hbm, g_v, local_sem.at[1])
    load_f = pltpu.make_async_copy(f_hbm.at[0], f_v.at[x, y, c], local_sem.at[2])
    load_f.start()
    load_m.start()
    load_g.start()

    barrier = pltpu.get_barrier_semaphore()
    peers = (
        [(at(xs[d], y, c), z) for d in (1, 3)]
        + [(at(x, ys[d], c), z) for d in range(1, NY)]
        + [(i, zs[d]) for d in range(1, NZ)]
        + [(other, z)]
    )
    for peer in peers:
        pl.semaphore_signal(barrier, inc=1, device_id=peer, device_id_type=MESH)
    pl.semaphore_wait(barrier, len(peers))

    load_f.wait()
    start(fy)
    load_m.wait()
    load_g.wait()

    def add_buffer(k, _):
        r = pl.ds(pl.multiple_of(k * 64, 64), 64)
        b_v[r, :] = (m_v[r, :].astype(F32) + g_v[r, :].astype(F32)).astype(BF16)
        return 0

    lax.fori_loop(0, ROWS // 64, add_buffer, 0)
    stores = [pltpu.make_async_copy(b_v, b_hbm, local_sem.at[3])]
    stores[0].start()
    landed(fy)
    start(fx[:4])
    fc[0].start()
    x_all_forward(fx)
    x_all_finish(fx, fc[1:])
    landed(fc)

    sk_v[...] = jnp.dot(b_v[...], f_v[...].reshape(COLS, RANK), preferred_element_type=F32)
    start(up[:2])
    start(down[:2])
    for s in range(1, 4):
        for h, (first, size) in enumerate(parts):
            part = pl.ds(first, size)
            up[2 * s - 2 + h].wait_recv()
            mine = pl.ds(pl.multiple_of(zs[4 - s] * ZR + first, 8), size)
            up_v[s - 1, part, :] = up_v[s - 1, part, :] + sk_v[mine, :]
            up[2 * s + h].start()
            if s < 3:
                down[2 * s - 2 + h].wait_recv()
                mine = pl.ds(pl.multiple_of(zs[5 + s] * ZR + first, 8), size)
                dn_v[s - 1, part, :] = dn_v[s - 1, part, :] + sk_v[mine, :]
                down[2 * s + h].start()
    landed(down[4:])
    landed(up[6:])
    total = sk_v[pl.ds(pl.multiple_of(z * ZR, 8), ZR), :] + (up_v[3] + dn_v[2])
    so_v[...] = total
    sg_up[0].start()
    sg_down[0].start()
    sa_v[pl.ds(pl.multiple_of(z * ZR, 8), ZR), :] = total

    def sg_forward(s):
        sg_up[s - 1].wait_recv()
        sg_up[s].start()
        if s < 3:
            sg_down[s - 1].wait_recv()
            sg_down[s].start()

    def panels(core, out):
        for j in range(3):
            n = 3 * core + j
            last = n // 4
            r = pl.ds(pl.multiple_of(256 * last, 256), 256)
            q = pl.ds(pl.multiple_of(128 * n - 256 * last, 128), 128)
            out[256 * j : 256 * j + 256, :] = dot_tn(so_v[:, r], so_v[:, q], HI)

    panels(1 - c, gs_v)
    start(gc)
    panels(c, gm_v)
    landed(gc)
    gm_v[...] = gm_v[...] + gcr_v[...]
    start(gx[:4])
    sg_forward(1)
    x_sums_forward(gx, gm_v, GX, gxr_v)
    sg_forward(2)
    x_sums_finish(gx, gm_v, GX, gxr_v, g1_v)
    start(gy)
    sg_forward(3)
    total = g1_v[pl.ds(pl.multiple_of(y * GY, 8), GY), :]
    for d in range(1, NY):
        gy[d - 1].wait_recv()
        total = total + gyr_v[d - 1]
    gzr_v[z] = total
    start(gz)

    landed(sg_up[3:])
    landed(sg_down[2:])
    sh_v[...], sl_v[...] = split(sa_v[...])

    def project(half, j):
        cols = pl.ds(pl.multiple_of(half * 512, 512), 512)
        part = slice(HR * j, HR * j + HR)
        return dot_tn(b_v[:, cols], sh_v[:, part]) + dot_tn(b_v[:, cols], sl_v[:, part])

    for j in range(2):
        ps_v[j] = project(1 - c, j)
        start(pc[j])
    for j in range(2):
        pm_v[j] = project(c, j)
    landed(gz)
    total = gzr_v[0]
    for d in range(1, NZ):
        total = total + gzr_v[d]
    gg_v[pl.ds(pl.multiple_of(c * GC + x * GX + y * GY, 8), GY), :] = total
    start(hy)

    def px_start(j):
        landed(pc[j])
        pm_v[j] = pm_v[j] + pcr_v[j]
        start(px[j][:4])

    def px_forward(j):
        x_sums_forward(px[j], pm_v.at[j], 128, pxr_v.at[j])

    def px_finish(j):
        x_sums_finish(px[j], pm_v.at[j], 128, pxr_v.at[j], p1_v.at[j])
        start(py[j])

    def py_finish(j):
        total = p1_v[j, pl.ds(pl.multiple_of(y * 16, 16), 16), :]
        for d in range(1, NY):
            py[j][d - 1].wait_recv()
            total = total + pyr_v[j, d - 1]
        pf_v[j, pl.ds(pl.multiple_of(c * 512 + x * 128 + y * 16, 16), 16), :] = total
        start(qy[j])

    def qy_finish(j):
        landed(qy[j])
        start(qx[j][:4])
        qc[j][0].start()

    px_start(0)
    px_start(1)
    px_forward(0)
    landed(hy)
    start(hx[:4])
    hc[0].start()
    px_forward(1)
    x_all_forward(hx)
    px_finish(0)
    x_all_finish(hx, hc[1:])
    px_finish(1)
    landed(hc)

    steps = (
        (0, 3, lambda: py_finish(0)),
        (1, 0, lambda: py_finish(1)),
        (1, 9, lambda: qy_finish(0)),
        (2, 6, lambda: x_all_forward(qx[0])),
        (2, 7, lambda: qy_finish(1)),
        (2, 14, lambda: x_all_finish(qx[0], qc[0][1:])),
        (3, 6, lambda: x_all_forward(qx[1])),
        (3, 14, lambda: x_all_finish(qx[1], qc[1][1:])),
    )

    nb = RANK // 128

    ch_v[256:, :256] = jnp.zeros((256, 256), F32)
    for j, (r, q) in enumerate(PANELS):
        ch_v[r : r + 256, q : q + 128] = gg_v[256 * j : 256 * j + 256, :]
    r128 = lax.broadcasted_iota(jnp.int32, (128, 128), 0)
    c128 = lax.broadcasted_iota(jnp.int32, (128, 128), 1)

    def eliminate(k, _):
        mine = pl.ds(pl.multiple_of(k * 128, 128), 128)
        blk = ch_v[mine, mine]

        def between(j):
            for outer, pivot, step in steps:
                if j == pivot:
                    pl.when(k == outer)(step)

        done = diag_inverse([blk[8 * j : 8 * j + 8, :] for j in range(16)], between)
        linv = jnp.where(r128 >= c128, jnp.concatenate(done, axis=0), 0.0)
        ch_v[mine, mine] = jnp.where(r128 == c128, 1.0, 0.0)
        ch_v[mine, :] = jnp.dot(linv, ch_v[mine, :], precision=HI, preferred_element_type=F32)
        for kk in range(nb - 1):

            @pl.when(k == kk)
            def _():
                lo, hi = 128 * kk, 128 * (kk + 1)
                ch_v[hi:, lo:hi] = jnp.zeros((RANK - hi, 128), F32)
                ch_v[hi:, :] = ch_v[hi:, :] - dot_tn(ch_v[lo:hi, hi:], ch_v[lo:hi, :], HI)

        return 0

    lax.fori_loop(0, nb, eliminate, 0)
    rr = lax.broadcasted_iota(jnp.int32, (RANK, RANK), 0)
    cc = lax.broadcasted_iota(jnp.int32, (RANK, RANK), 1)
    xh_v[...], xl_v[...] = split(jnp.where(rr >= cc, ch_v[...], 0.0))

    def times_inverse(hi, lo):
        return dot_nt(hi, xh_v[...]) + (dot_nt(hi, xl_v[...]) + dot_nt(lo, xh_v[...]))

    def store(src, dst, sem):
        stores.append(pltpu.make_async_copy(src, dst, local_sem.at[sem]))
        stores[-1].start()

    def projected(half):
        r = pl.ds(pl.multiple_of(half * 512, 512), 512)
        proj = times_inverse(*split(jnp.concatenate([pf_v[0, r, :], pf_v[1, r, :]], axis=1)))
        pr_v[r, :] = proj
        ph_v[r, :] = proj.astype(BF16)
        return jnp.sum((proj * proj).reshape(64, 8, RANK), axis=0)

    squares = projected(c)
    landed(qc[0])
    landed(qc[1])
    squares = jnp.sum(squares + projected(1 - c), axis=0, keepdims=True)
    for j in range(4):
        nz_v[z, j : j + 1, :] = squares[:, 128 * j : 128 * j + 128]
    nz_v[z, 4:8, :] = jnp.zeros((4, 128), F32)
    start(nz)
    store(ph_v, ph_hbm, 5)
    left = times_inverse(sh_v[...], sl_v[...])
    le_v[...] = left
    lh_v[...] = left.astype(BF16)
    store(lh_v, lh_hbm, 4)

    for copies in (fy, fx, fc, up, down, sg_up, sg_down, gc, gx, gy, gz, hy, hx, hc, *pc, *px, *py, *qy, *qx, *qc):
        for k in copies:
            k.wait_send()
    landed(nz)
    total = nz_v[0]
    for d in range(1, NZ):
        total = total + nz_v[d]
    inv = 1.0 / jnp.sqrt(total + 1e-06)
    inv = jnp.concatenate([inv[j : j + 1, :] for j in range(4)], axis=1)
    sc_v[...] = (le_v[...] * inv).astype(BF16)
    store(sc_v, sc_hbm, 6)
    fo_v[0] = (pr_v[pl.ds(pl.multiple_of(i * SHARE, SHARE), SHARE), :] * inv).astype(BF16)
    store(fo_v, fo_hbm, 7)

    for k in nz:
        k.wait_send()
    for k in stores:
        k.wait()


def finish(b_ref, w_ref, lh_ref, sc_ref, ph_ref, f_ref, mo_ref, wo_ref, fo_ref):
    approx = dot_nt(lh_ref[...], ph_ref[...])
    mo_ref[...] = (b_ref[...].astype(F32) - 0.05 * approx).astype(BF16)
    update = dot_nt(sc_ref[...], ph_ref[...])
    scale = 0.2 * (FF * D / RANK) ** 0.5
    wo_ref[...] = (w_ref[...].astype(F32) - scale * update).astype(BF16)
    fo_ref[...] = f_ref[...]


def local(momentum, gradient, right_factor, weight):
    any_spec = pl.BlockSpec(memory_space=pl.ANY)
    v = pltpu.VMEM
    buffer, left_half, scaled_half, projected_half, factor_new = pl.pallas_call(
        kernel,
        out_shape=(
            jax.ShapeDtypeStruct((ROWS, COLS), BF16),
            jax.ShapeDtypeStruct((ROWS, RANK), BF16),
            jax.ShapeDtypeStruct((ROWS, RANK), BF16),
            jax.ShapeDtypeStruct((COLS, RANK), BF16),
            jax.ShapeDtypeStruct((1, SHARE, RANK), BF16),
        ),
        in_specs=[any_spec] * 3,
        out_specs=(any_spec,) * 5,
        scratch_shapes=[
            v((ROWS, COLS), BF16), v((ROWS, COLS), BF16), v((ROWS, COLS), BF16),
            v((NX, NY, NC, SHARE, RANK), BF16),
            v((ROWS, RANK), F32), v((4, ZR, RANK), F32), v((3, ZR, RANK), F32), v((ZR, RANK), F32), v((ROWS, RANK), F32),
            v((ROWS, RANK), BF16), v((ROWS, RANK), BF16),
            v((GC, 128), F32), v((GC, 128), F32), v((GC, 128), F32),
            v((6, GX // 2, 128), F32), v((GX, 128), F32), v((7, GY, 128), F32), v((8, GY, 128), F32),
            v((2 * GC, 128), F32), v((RANK, RANK), F32),
            v((2, 512, HR), F32), v((2, 512, HR), F32), v((2, 512, HR), F32),
            v((2, 6, 64, HR), F32), v((2, 128, HR), F32), v((2, 7, 16, HR), F32), v((2, COLS, HR), F32),
            v((COLS, RANK), F32),
            v((RANK, RANK), BF16), v((RANK, RANK), BF16),
            v((ROWS, RANK), F32), v((ROWS, RANK), BF16), v((ROWS, RANK), BF16), v((COLS, RANK), BF16),
            v((8, 8, 128), F32), v((1, SHARE, RANK), BF16),
            pltpu.SemaphoreType.DMA((N_SEMS,)),
            pltpu.SemaphoreType.DMA((N_SEMS,)),
            pltpu.SemaphoreType.DMA((8,)),
        ],
        compiler_params=pltpu.CompilerParams(
            collective_id=0, has_side_effects=True, vmem_limit_bytes=60 * 2**20
        ),
        name="dion_step",
    )(momentum, gradient, right_factor)
    tile = 512
    wide_spec = pl.BlockSpec((ROWS, tile), lambda j: (0, j))
    left_spec = pl.BlockSpec((ROWS, RANK), lambda j: (0, 0))
    share_spec = pl.BlockSpec((1, SHARE, RANK), lambda j: (0, 0, 0))
    momentum_new, weight_new, factor_new = pl.pallas_call(
        finish,
        grid=(COLS // tile,),
        out_shape=(
            jax.ShapeDtypeStruct((ROWS, COLS), BF16),
            jax.ShapeDtypeStruct((ROWS, COLS), BF16),
            jax.ShapeDtypeStruct((1, SHARE, RANK), BF16),
        ),
        in_specs=[
            wide_spec, wide_spec, left_spec, left_spec,
            pl.BlockSpec((tile, RANK), lambda j: (j, 0)), share_spec,
        ],
        out_specs=(wide_spec, wide_spec, share_spec),
        compiler_params=pltpu.CompilerParams(vmem_limit_bytes=60 * 2**20),
        name="finish",
    )(buffer, weight, left_half, scaled_half, projected_half, factor_new)
    return momentum_new, factor_new, weight_new


def solution(mesh):
    return jax.shard_map(
        local,
        mesh=mesh,
        in_specs=(P("fsdp", "tp"), P("fsdp", "tp"), P("tp", "fsdp", None), P("fsdp", "tp")),
        out_specs=(P("fsdp", "tp"), P("tp", "fsdp", None), P("fsdp", "tp")),
        check_vma=False,
    )
```
